32 devices in a mesh: dp: 4 (over y, core), expert: 8 (over z, x).
Axes of the slice: x: 2, y: 2, z: 4, core: 2. Of those that a mesh axis runs over, the one named last changes fastest.
Arguments:
- tokens: bfloat16 [4096, 2048], P(('dp', 'expert')), may hold values from -6 to 6
- grad_out: bfloat16 [4096, 2048], P(('dp', 'expert')), may hold values from -6 to 6
- routes: int32 [4096, 3], P(('dp', 'expert')), may hold values from 0 to 7, all different within a row; in each aligned block of 128 rows (0 to 127, 128 to 255, ...) at most 64 rows name the same one
- route_weight: bfloat16 [4096, 3], P(('dp', 'expert')), may hold values from 0.099609375 to 1
- w_gate: bfloat16 [8, 2048, 1408], P('expert'), may hold values from -0.125 to 0.125
- w_up: bfloat16 [8, 2048, 1408], P('expert'), may hold values from -0.125 to 0.125
- w_down: bfloat16 [8, 1408, 2048], P('expert'), may hold values from -0.15625 to 0.15625
Outputs:
- token_grad: bfloat16 [4096, 2048], P(('dp', 'expert'))
- prob_grad: bfloat16 [4096, 3], P(('dp', 'expert'))
- wgrad_gate: bfloat16 [8, 2048, 1408], P('expert', 'dp')
- wgrad_up: bfloat16 [8, 2048, 1408], P('expert', 'dp')
- wgrad_down: bfloat16 [8, 1408, 2048], P('expert', None, 'dp')
The draws below stay inside these ranges and needn't reach their ends.
Inputs may be any that keep to these rules, and one draw needn't show every extreme that they name: In each aligned block of 128 tokens (the tokens of one device) no expert is named by more than 64 routes, a bound that some block reaches; the 3 routes of a token name different experts.
All inputs are finite; a program needn't handle non-finite values.
Results may differ from the reference program's by a relative error of at most 0.014.
Values may be sent and summed in bfloat16 or wider, within the bound.
No kernel may reach another device: no remote copies, remote signals or barrier semaphores. Data moves between devices by JAX's collectives and lax.ppermute only.
A program may use at most 128 MiB of HBM per device.

```python
import math
import jax
import jax.numpy as jnp
import numpy as np
from jax import lax

D = 2048
FF = 1408
TOP = 3
TOK_DEV = 128
EXPERTS = 8
CAP = 64
TOKENS = 4096
N_DP = 4
N_EXPERT = 8


def strengthened(values, stream_key, source, target, blocks, factor):
    def block_of(dim):
        return (jnp.arange(values.shape[dim]) // (values.shape[dim] // blocks)).reshape((-1,) + (1,) * (values.ndim - 1 - dim))

    first = jax.random.permutation(stream_key, blocks)[block_of(target)]
    other_side = (block_of(target) + blocks // 2) % blocks
    return jnp.where((block_of(source) == first) | (block_of(source) == other_side), factor * values, values)


def level_of(rng, shape, split, smallest, top_value):
    loudness, own = 1.0, jax.random.fold_in(rng, 6)
    for axis_at, shards_of in split:
        heights = jnp.exp(jax.random.uniform(jax.random.fold_in(own, axis_at), (shards_of,), jnp.float32, smallest / len(split), top_value / len(split)))
        loudness = loudness * jnp.repeat(heights, shape[axis_at] // shards_of).reshape([-1 if axis == axis_at else 1 for axis in range(len(shape))])
    return loudness


def deal_out(stream_key, own, number, rows, count, top, limit, slope):
    ranking = jax.random.permutation(stream_key, count)
    crowded, common = portions_of(count, rows * top, limit, slope, True), portions_of(count, rows * top, limit, slope, False)
    places = jnp.arange(count)

    def named(lengths, turn):
        used = int((lengths > 0).sum())
        fixed = max(1, used // 4)
        moved = fixed + (places - fixed + turn * (used - fixed)) % max(1, count - fixed)
        return jnp.zeros((count,), jnp.int32).at[ranking[jnp.where(places < fixed, places, moved)]].set(jnp.asarray(lengths, jnp.int32))

    lengths = jnp.where(number % 4 == 0, named(crowded, number // 4), named(common, number - number // 4 - 1))
    mixed = jax.random.permutation(jax.random.fold_in(own, 3), count)
    giver, sink = mixed[0:count // 2 * 2:2], mixed[1:count // 2 * 2:2]
    room = jnp.minimum(lengths[giver] - 1, limit - lengths[sink]) // 2
    room = jnp.where((giver == ranking[0]) | (sink == ranking[0]) | (lengths[sink] == 0), 0, jnp.maximum(room, 0))
    moved = jax.random.randint(jax.random.fold_in(own, 4), (count // 2,), 0, 1 << 20) % (room + 1)
    lengths = lengths.at[giver].add(-moved).at[sink].add(moved)
    members = jnp.searchsorted(jnp.cumsum(lengths), jnp.arange(rows * top), side="right").astype(jnp.int32)
    table = members.reshape(top, rows).T
    table = table[jax.random.permutation(jax.random.fold_in(own, 1), rows)]
    turn = jax.random.randint(jax.random.fold_in(own, 2), (rows, 1), 0, top)
    return jnp.take_along_axis(table, (jnp.arange(top)[None, :] + turn) % top, axis=1)


def portions_of(count, total, limit, slope, full):
    weights = [(1 << 20) // math.isqrt(standing ** slope) + 1 for standing in range(1, count + 1)]
    largest = limit if full else min(limit, max(-(-total // count), total * weights[0] // sum(weights)))
    least = 1 if total - largest >= count - 1 else 0
    holding, rest = [largest] + [least] * (count - 1), total - largest - least * (count - 1)
    while rest > 0:
        movable = [i for i in range(1, count) if holding[i] < largest] or [i for i in range(1, count) if holding[i] < limit]
        whole, left = sum([weights[i] for i in movable]), rest
        for i in movable:
            extra = min(limit - holding[i], max(1, left * weights[i] // whole), rest)
            holding[i] = holding[i] + extra
            rest = rest - extra
    return np.array(holding)


def gaussian(key, dims, width, most, pieces=(), held_as=jnp.bfloat16):
    result = jax.random.normal(key, dims, jnp.float32) * width
    if len(pieces) > 0:
        result = level_of(key, dims, pieces, -0.22, 0.18) * result
    return jnp.clip(result, min=-most, max=most).astype(held_as)


def gaussian_with(rng, dims, width, most, cuts, heavy, held_as=jnp.bfloat16):
    entries = width * jax.random.normal(rng, dims, jnp.float32)
    if cuts:
        entries = entries * level_of(rng, dims, cuts, -0.22, 0.18)
    return jnp.clip(strengthened(entries, jax.random.fold_in(rng, 3), *heavy), -most, most).astype(held_as)


def setup_inputs(seed: int = 0) -> dict:
    key_list = jax.random.split(jax.random.key(seed), 8)
    tokens = gaussian(key_list[0], (TOKENS, D), 1.0, 6.0, ((0, 32),))
    grad_out = gaussian_with(key_list[1], (TOKENS, D), 1.0, 6.0, ((0, 32),), (0, 1, 32, 2.75))
    routes_keys = jax.random.split(jax.random.fold_in(key_list[2], 1), TOKENS // TOK_DEV)
    routes_turns = jax.random.permutation(jax.random.fold_in(key_list[2], 3), TOKENS // TOK_DEV)
    routes = jax.vmap(lambda own, number: deal_out(jax.random.fold_in(key_list[2], 2), own, number, TOK_DEV, EXPERTS, TOP, CAP, 2))(routes_keys, routes_turns).reshape((TOKENS, TOP))
    route_weight = jnp.clip(jnp.exp(math.log(1.0) - 2.306499 * jax.random.uniform(key_list[3], (TOKENS, TOP), jnp.float32) ** level_of(key_list[3], (TOKENS, TOP), ((0, 32),), -0.2, 0.2)), 0.099609375, 1.0).astype(jnp.bfloat16)
    w_gate = gaussian(key_list[4], (EXPERTS, D, FF), D ** -0.5, 0.125, ((0, 8),))
    w_up = gaussian(key_list[5], (EXPERTS, D, FF), D ** -0.5, 0.125, ((0, 8),))
    w_down = gaussian(key_list[6], (EXPERTS, FF, D), FF ** -0.5, 0.15625, ((0, 8),))
    return dict(tokens=tokens, grad_out=grad_out, routes=routes, route_weight=route_weight, w_gate=w_gate, w_up=w_up, w_down=w_down)


def expert_rows(got_tokens, got_grads, got_weights, gate_mat, up_mat, down_mat):
    pre_gate = jnp.dot(got_tokens, gate_mat, preferred_element_type=jnp.float32)
    pre_up = jnp.dot(got_tokens, up_mat, preferred_element_type=jnp.float32)
    sigma = jax.nn.sigmoid(pre_gate)
    active = pre_gate * sigma
    hidden = (active * pre_up).astype(jnp.bfloat16)
    output = jnp.dot(hidden, down_mat, preferred_element_type=jnp.float32)
    prob_grad = jnp.sum(got_grads.astype(jnp.float32) * output, axis=1).astype(jnp.bfloat16)
    scaled = (got_weights.astype(jnp.float32)[:, None] * got_grads.astype(jnp.float32)).astype(jnp.bfloat16)
    hidden_grad = jnp.dot(scaled, down_mat.T, preferred_element_type=jnp.float32)
    gate_grad = (hidden_grad * pre_up * sigma * (1.0 + pre_gate * (1.0 - sigma))).astype(jnp.bfloat16)
    up_grad = (hidden_grad * active).astype(jnp.bfloat16)
    input_grad = jnp.dot(gate_grad, gate_mat.T, preferred_element_type=jnp.float32)
    input_grad = (input_grad + jnp.dot(up_grad, up_mat.T, preferred_element_type=jnp.float32)).astype(jnp.bfloat16)
    return input_grad, prob_grad, hidden, scaled, gate_grad, up_grad


def rounded_sum(partials):
    kept = lax.optimization_barrier(partials.astype(jnp.bfloat16))
    return jnp.sum(kept.astype(jnp.float32), axis=0).astype(jnp.bfloat16)


def reference(tokens, grad_out, routes, route_weight, w_gate, w_up, w_down):
    devices = N_DP * N_EXPERT
    flat_ids = routes.reshape(devices, TOK_DEV * TOP)
    onehot = (flat_ids[:, :, None] == jnp.arange(EXPERTS, dtype=jnp.int32)[None, None, :]).astype(jnp.int32)
    before = jnp.cumsum(onehot, axis=1) - onehot
    slot_pos = jnp.sum(before * onehot, axis=2).astype(jnp.int32)
    column = (jnp.arange(devices, dtype=jnp.int32)[:, None] * CAP + slot_pos).reshape(-1)
    expert = flat_ids.reshape(-1)
    slot_span = devices * CAP
    token_rep = jnp.repeat(tokens, TOP, axis=0)
    grad_rep = jnp.repeat(grad_out, TOP, axis=0)
    buf_tokens = jnp.zeros((EXPERTS, slot_span, D), jnp.bfloat16).at[expert, column].set(token_rep)
    buf_grads = jnp.zeros((EXPERTS, slot_span, D), jnp.bfloat16).at[expert, column].set(grad_rep)
    buf_weights = jnp.zeros((EXPERTS, slot_span), jnp.bfloat16).at[expert, column].set(route_weight.reshape(-1))
    row_group = N_EXPERT * CAP

    def one_expert(bundle):
        got_tokens, got_grads, got_weights, gate_mat, up_mat, down_mat = bundle
        input_grad, prob_grad, hidden, scaled, gate_grad, up_grad = expert_rows(
            got_tokens, got_grads, got_weights, gate_mat, up_mat, down_mat)
        token_blocks = got_tokens.reshape(N_DP, row_group, D).astype(jnp.float32)
        scaled_blocks = scaled.reshape(N_DP, row_group, D).astype(jnp.float32)
        hidden_blocks = hidden.reshape(N_DP, row_group, FF).astype(jnp.float32)
        part_gate = jnp.einsum("nsd,nsf->ndf", token_blocks, gate_grad.reshape(N_DP, row_group, FF).astype(jnp.float32))
        part_up = jnp.einsum("nsd,nsf->ndf", token_blocks, up_grad.reshape(N_DP, row_group, FF).astype(jnp.float32))
        part_down = jnp.einsum("nsf,nsd->nfd", hidden_blocks, scaled_blocks)
        return input_grad, prob_grad, rounded_sum(part_gate), rounded_sum(part_up), rounded_sum(part_down)

    results = lax.map(one_expert, (buf_tokens, buf_grads, buf_weights, w_gate, w_up, w_down))
    route_grad = results[0][expert, column]
    token_grad = jnp.sum(route_grad.reshape(TOKENS, TOP, D).astype(jnp.float32), axis=1).astype(jnp.bfloat16)
    prob_grad = results[1][expert, column].reshape(TOKENS, TOP)
    return token_grad, prob_grad, results[2], results[3], results[4]
```

```python
import jax
import jax.numpy as jnp
from jax import lax
from jax.sharding import PartitionSpec as P

BF = jnp.bfloat16
F32 = jnp.float32


def ring_order(count):
    inner = 2 if count <= 8 else 4
    outer = count // inner
    cycle = [row * inner for row in range(outer)]
    for row in reversed(range(outer)):
        columns = list(range(1, inner))
        if (outer - 1 - row) % 2:
            columns.reverse()
        cycle += [row * inner + column for column in columns]
    return cycle


def right_product(left, right):
    return lax.dot_general(left, right, (((1,), (1,)), ((), ())), preferred_element_type=F32)


def left_product(left, right):
    return lax.dot_general(left, right, (((0,), (0,)), ((), ())), preferred_element_type=F32)


def product(left, right):
    return jnp.dot(left, right, preferred_element_type=F32)


def forward_rows(rows, gate_mat, up_mat):
    pre_gate = product(rows, gate_mat)
    pre_up = product(rows, up_mat)
    sigma = jax.nn.sigmoid(pre_gate)
    active = pre_gate * sigma
    slope = pre_up * sigma * (1.0 + pre_gate * (1.0 - sigma))
    return active.astype(BF), slope.astype(BF), (active * pre_up).astype(BF)


def backward_rows(grads, weights, active, slope, hidden, down_mat):
    plain = right_product(grads, down_mat)
    hidden = hidden.astype(F32)
    prob = jnp.sum(hidden * plain, axis=1)
    hidden_grad = weights * plain
    gate_grad = (hidden_grad * slope.astype(F32)).astype(BF)
    up_grad = (hidden_grad * active.astype(F32)).astype(BF)
    return gate_grad, up_grad, (weights * hidden).astype(BF), prob


def body(tokens, grad_out, routes, route_weight, w_gate, w_up, w_down):
    tok_rows, model_width = tokens.shape
    route_count = routes.shape[1]
    experts = lax.axis_size("expert")
    copies = lax.axis_size("dp")
    mirrors = copies // 2
    half_ring = experts // 2
    capacity = 4 * tok_rows * route_count // (3 * experts)
    share = model_width // copies
    gate_mat, up_mat, down_mat = w_gate[0], w_up[0], w_down[0]
    ring = ring_order(experts)
    ahead = [(ring[i], ring[(i + 1) % experts]) for i in range(experts)]
    behind = [(ring[i], ring[(i - 1) % experts]) for i in range(experts)]
    place_of = [ring.index(i) for i in range(experts)]
    here = jnp.array(place_of, jnp.int32)[lax.axis_index("expert")]
    copy_here = lax.axis_index("dp")

    offsets = [0]
    for step in range(1, half_ring):
        offsets += [-step, step]
    offsets.append(half_ring)
    sources = jnp.array(ring, jnp.int32)[(here + jnp.array(offsets, jnp.int32)) % experts]

    expert_ids = jnp.arange(experts, dtype=jnp.int32)
    named = routes[:, :, None] == expert_ids[None, None, :]
    dense_weight = jnp.sum(jnp.where(named, route_weight[:, :, None].astype(F32), 0.0), axis=1)
    sent_weight = dense_weight.T.astype(BF).reshape(experts, 1, tok_rows)

    streams = [[tokens], [grad_out]]
    moving = [[tokens, tokens], [grad_out, grad_out]]
    got_weight = lax.all_to_all(sent_weight, "expert", split_axis=0, concat_axis=0, tiled=True)
    for step in range(1, half_ring):
        for which in range(2):
            moving[which][0] = lax.ppermute(moving[which][0], "expert", ahead)
            moving[which][1] = lax.ppermute(moving[which][1], "expert", behind)
            streams[which] += moving[which]
    mid = tok_rows // 2
    for which in range(2):
        first = lax.ppermute(moving[which][0][:mid], "expert", ahead)
        second = lax.ppermute(moving[which][1][mid:], "expert", behind)
        streams[which].append(jnp.concatenate([first, second], axis=0))

    weight_of = got_weight.reshape(experts, tok_rows)[sources]
    routed = weight_of > 0
    token_ids = jnp.arange(tok_rows, dtype=jnp.int32)
    earlier = (token_ids[:, None] < token_ids[None, :]).astype(BF)
    slot = product(routed.astype(BF), earlier).astype(jnp.int32)
    slot = jnp.where(routed, slot, -1)
    pick = (slot[:, None, :] == jnp.arange(capacity, dtype=jnp.int32)[None, :, None]).astype(BF)
    slot_weight = jnp.sum(pick.astype(F32) * weight_of[:, None, :].astype(F32), axis=2)
    slot_weight = slot_weight.reshape(experts * capacity, 1)

    cuts = [0, 3, 5, experts] if experts == 8 else [0, experts // 2, experts]
    mirror_maps = [
        [(d, (d + 2 * turn) % copies) for d in range(copies)] for turn in range(1, mirrors)
    ]
    own, others = [[], []], [[[] for _ in mirror_maps] for _ in range(2)]
    for low, high in zip(cuts[:-1], cuts[1:]):
        for which in range(2):
            rows = jnp.concatenate(
                [product(pick[j], streams[which][j]).astype(BF) for j in range(low, high)], axis=0
            )
            own[which].append(rows)
            for turn, pairs in enumerate(mirror_maps):
                others[which][turn].append(lax.ppermute(rows, "dp", pairs))
    other_weight = [
        lax.ppermute(slot_weight.astype(BF), "dp", pairs).astype(F32) for pairs in mirror_maps
    ]

    late = cuts[-2]
    parts = []
    for low, high, pieces in ((0, late, slice(0, -1)), (late, experts, slice(-1, None))):
        rows = jnp.concatenate(own[0][pieces], axis=0)
        grads = jnp.concatenate(own[1][pieces], axis=0)
        acts = forward_rows(rows, gate_mat, up_mat)
        weights = slot_weight[low * capacity : high * capacity]
        gate_grad, up_grad, weighted, prob = backward_rows(grads, weights, *acts, down_mat)
        back = right_product(gate_grad, gate_mat) + right_product(up_grad, up_mat)
        parts.append((rows, grads, gate_grad, up_grad, weighted, prob, back.astype(BF)))

    def dense_back(index):
        part, at = (0, index) if index < late else (1, index - late)
        rows = parts[part][6][at * capacity : (at + 1) * capacity]
        return left_product(pick[index], rows)

    width = model_width // 2
    at_offset = {offset: index for index, offset in enumerate(offsets)}
    far = dense_back(at_offset[half_ring]).astype(BF)
    totals = []
    columns = [slice(0, width), slice(width, model_width)]
    run = [[far[:mid, c], far[mid:, c]] for c in columns]
    for step in range(half_ring - 1, -1, -1):
        for which, c in enumerate(columns):
            for side, pairs in enumerate((ahead, behind)):
                run[which][side] = lax.ppermute(run[which][side], "expert", pairs)
        if step == half_ring - 1:
            edge = ((0, tok_rows - mid), (0, 0)), ((mid, 0), (0, 0))
            run = [
                [jnp.pad(run[which][side], edge[side]) for side in range(2)] for which in range(2)
            ]
        if step > 0:
            for side, sign in enumerate((1, -1)):
                term = dense_back(at_offset[sign * step])
                for which, c in enumerate(columns):
                    run[which][side] = (run[which][side].astype(F32) + term[:, c]).astype(BF)
    own_term = dense_back(0)
    token_grad = jnp.concatenate(
        [
            (run[w][0].astype(F32) + run[w][1].astype(F32) + own_term[:, c]).astype(BF)
            for w, c in enumerate(columns)
        ],
        axis=1,
    )

    prob = jnp.concatenate([part[5] for part in parts], axis=0).reshape(experts, 1, capacity)
    prob = jnp.sum(prob.reshape(experts, capacity, 1) * pick.astype(F32), axis=1)
    match = (sources[:, None] == expert_ids[None, :]).astype(F32)
    prob = jnp.sum(match[:, :, None] * prob[:, None, :], axis=0)
    back_prob = lax.all_to_all(
        prob.astype(BF).reshape(experts, 1, tok_rows), "expert", split_axis=0, concat_axis=0, tiled=True
    ).reshape(experts, tok_rows)
    prob_out = jnp.sum(jnp.where(named, back_prob.T[:, None, :].astype(F32), 0.0), axis=2).astype(BF)

    all_parts = [part[:5] for part in parts]
    for turn in range(mirrors - 1):
        rows = jnp.concatenate(others[0][turn], axis=0)
        grads = jnp.concatenate(others[1][turn], axis=0)
        acts = forward_rows(rows, gate_mat, up_mat)
        gate_grad, up_grad, weighted, _ = backward_rows(grads, other_weight[turn], *acts, down_mat)
        all_parts.append((rows, grads, gate_grad, up_grad, weighted))
    rows, grads, gate_grad, up_grad, weighted = (
        jnp.concatenate([part[i] for part in all_parts], axis=0) for i in range(5)
    )

    core_pairs = [(d, d ^ 1) for d in range(copies)]

    def shares(copy):
        cut_rows = lax.dynamic_slice_in_dim(rows, copy * share, share, axis=1)
        cut_grads = lax.dynamic_slice_in_dim(grads, copy * share, share, axis=1)
        return (
            left_product(cut_rows, gate_grad),
            left_product(cut_rows, up_grad),
            left_product(weighted, cut_grads),
        )

    given = [lax.ppermute(s.astype(BF), "dp", core_pairs) for s in shares(copy_here ^ 1)]
    kept = shares(copy_here)
    wgrads = [(k + g.astype(F32)).astype(BF)[None] for k, g in zip(kept, given)]
    return (token_grad, prob_out, *wgrads)


def solution(mesh):
    in_specs = (
        P(("dp", "expert"), None),
        P(("dp", "expert"), None),
        P(("dp", "expert"), None),
        P(("dp", "expert"), None),
        P("expert", None, None),
        P("expert", None, None),
        P("expert", None, None),
    )
    out_specs = (
        P(("dp", "expert"), None),
        P(("dp", "expert"), None),
        P("expert", "dp", None),
        P("expert", "dp", None),
        P("expert", None, "dp"),
    )
    return jax.shard_map(body, mesh=mesh, in_specs=in_specs, out_specs=out_specs, check_vma=False)
```

```python
import functools
import math

import jax
import jax.numpy as jnp
from jax import lax
from jax.experimental import pallas as pl
from jax.experimental.pallas import tpu as pltpu
from jax.sharding import PartitionSpec as P

BF = jnp.bfloat16
F32 = jnp.float32
LANES = 128
TILE = 256
MIB = 1024 * 1024


def ring_order(count):
    inner = 2 if count <= 8 else 4
    outer = count // inner
    cycle = [row * inner for row in range(outer)]
    for row in reversed(range(outer)):
        columns = list(range(1, inner))
        if (outer - 1 - row) % 2:
            columns.reverse()
        cycle += [row * inner + column for column in columns]
    return cycle


def product(left, right):
    return jnp.dot(left, right, preferred_element_type=F32)


def right_product(left, right):
    return lax.dot_general(left, right, (((1,), (1,)), ((), ())), preferred_element_type=F32)


def left_product(left, right):
    return lax.dot_general(left, right, (((0,), (0,)), ((), ())), preferred_element_type=F32)


ANY = pl.BlockSpec(memory_space=pl.ANY)
HELD = pl.BlockSpec(memory_space=pltpu.VMEM)
SCALAR = pl.BlockSpec(memory_space=pltpu.SMEM)


def far_shape(rows, columns):
    return pltpu.HBM((rows, columns), BF)


def shape_of(rows, columns, kind=BF):
    return jax.ShapeDtypeStruct((rows, columns), kind)


def cost(flops, moved):
    return pl.CostEstimate(flops=int(flops), bytes_accessed=int(moved), transcendentals=0)


def params(scratch, spare):
    held = [math.prod(one.shape) * 2 for one in scratch if one.memory_space == pltpu.VMEM]
    return pltpu.CompilerParams(vmem_limit_bytes=sum(held) + spare * MIB)


def far(array):
    return pltpu.with_memory_space_constraint(array, pltpu.HBM)


def after(value, *deps):
    if not deps:
        return value
    return lax.optimization_barrier((value, deps))[0]


def spans_of(width):
    return [(low, min(low + TILE, width)) for low in range(0, width, TILE)]


def copy_all(pairs, sems):
    copies = [pltpu.make_async_copy(a, b, sems.at[i]) for i, (a, b) in enumerate(pairs)]
    for copy in copies:
        copy.start()
    return copies


def wait_all(copies):
    for copy in copies:
        copy.wait()


class Outgoing:
    def __init__(self, sems):
        self.sems, self.copies = sems, []

    def send(self, source, target):
        copy = pltpu.make_async_copy(source, target, self.sems.at[len(self.copies)])
        copy.start()
        self.copies.append(copy)

    def wait(self):
        wait_all(self.copies)


def stacked(parts, into, columns=None):
    pairs, at = [], 0
    for part in parts:
        source = part if columns is None else part.at[:, columns]
        pairs.append((source, into.at[pl.ds(at, part.shape[0]), :]))
        at += part.shape[0]
    return pairs


def eye(size):
    first = lax.broadcasted_iota(jnp.int32, (size, size), 0)
    second = lax.broadcasted_iota(jnp.int32, (size, size), 1)
    return (first == second).astype(F32).astype(BF)


def load_kernel(*refs):
    count = (len(refs) - 1) // 2
    wait_all(copy_all(zip(refs[:count], refs[count : 2 * count]), refs[-1]))


def load_weights(*mats):
    return pl.pallas_call(
        load_kernel,
        out_shape=tuple(pltpu.VMEM(mat.shape, mat.dtype) for mat in mats),
        in_specs=[ANY] * len(mats),
        scratch_shapes=[pltpu.SemaphoreType.DMA((len(mats),))],
        compiler_params=params([], 2),
        cost_estimate=cost(0, 4 * sum(mat.size for mat in mats)),
        name="load_weights",
    )(*[far(mat) for mat in mats])


def pack_kernel(tokens, grads, routes, weights, out, held, turned, sems):
    rows, width = tokens.shape
    pairs = ((tokens, pl.ds(0, width)), (grads, pl.ds(width + LANES, width)))
    copies = copy_all([(part, held.at[:, band]) for part, band in pairs], sems)
    expert = lax.broadcasted_iota(jnp.int32, (LANES, rows), 0)
    dense = jnp.zeros((LANES, rows), F32)
    for k in range(routes.shape[0]):
        dense += jnp.where(routes[k : k + 1, :] == expert, weights[k : k + 1, :].astype(F32), 0.0)
    turned[...] = dense.astype(BF)
    held[:, width : width + LANES] = right_product(eye(rows), turned[...]).astype(BF)
    wait_all(copies)
    wait_all(copy_all([(held, out)], sems))


def pack(tokens, grads, routes, weights):
    rows, width = tokens.shape
    scratch = [
        pltpu.VMEM((rows, 2 * width + LANES), BF),
        pltpu.VMEM((LANES, rows), BF),
        pltpu.SemaphoreType.DMA((2,)),
    ]
    return pl.pallas_call(
        pack_kernel,
        out_shape=far_shape(rows, 2 * width + LANES),
        in_specs=[ANY, ANY, HELD, HELD],
        out_specs=ANY,
        scratch_shapes=scratch,
        compiler_params=params(scratch, 3),
        cost_estimate=cost(1e6, 8 * rows * width),
        name="pack",
    )(far(tokens), far(grads), routes.T, weights.T)


def pick_kernel(capacity, counts, halves, me, *refs):
    total = sum(counts)
    blocks, refs = refs[:total], refs[total:]
    rows_out, choice, refs = refs[0], refs[1], refs[2:]
    split, (held, made, sems, out_sems) = refs[:-4], refs[-4:]
    tok_rows = choice.shape[1]
    width = (held.shape[1] - LANES) // 2
    wide = width + LANES
    copies, at = [], 0
    for j, count in enumerate(counts):
        rows, low, pairs = pl.ds(j * tok_rows, tok_rows), 0, []
        for part in blocks[at : at + count]:
            pairs.append((part, held.at[rows, pl.ds(low, part.shape[1])]))
            low += part.shape[1]
        copies.append(copy_all(pairs, sems.at[j]))
        at += count
    lane = lax.broadcasted_iota(jnp.int32, (8, LANES), 1)
    mine = (lane == me[0]).astype(F32).astype(BF)
    first = lax.broadcasted_iota(jnp.int32, (tok_rows, tok_rows), 0)
    second = lax.broadcasted_iota(jnp.int32, (tok_rows, tok_rows), 1)
    earlier = (first < second).astype(F32).astype(BF)
    want = lax.broadcasted_iota(jnp.int32, (capacity, tok_rows), 0)
    sent = Outgoing(out_sems)
    for j in range(len(counts)):
        wait_all(copies[j])
        near = pl.ds(j * tok_rows, tok_rows)
        if halves:
            band = pl.ds(wide, width) if j else pl.ds(0, wide)
            sent.send(held.at[near, band], split[j])
        out = pl.ds(j * capacity, capacity)
        block = held[near, :]
        routed = right_product(mine, block[:, width:wide]) > 0
        slot = product(routed.astype(F32).astype(BF), earlier)
        slot = jnp.where(routed, slot, -1.0).astype(jnp.int32)
        pick = (want == slot[0:1, :]).astype(F32).astype(BF)
        choice[out, :] = pick
        made[out, :] = product(pick, block).astype(BF)
        sent.send(made.at[out, :], rows_out.at[out, :])
    sent.wait()


def pick_rows(me, capacity, blocks, halves=False):
    counts = [len(parts) for parts in blocks]
    flat = [part for parts in blocks for part in parts]
    wide = sum(part.shape[1] for part in blocks[0])
    tok_rows = flat[0].shape[0]
    rows = capacity * len(blocks)
    width = (wide - LANES) // 2
    out_shape = [far_shape(rows, wide), shape_of(rows, tok_rows)]
    if halves:
        out_shape += [far_shape(tok_rows, width + LANES), far_shape(tok_rows, width)]
    scratch = [
        pltpu.VMEM((tok_rows * len(blocks), wide), BF),
        pltpu.VMEM((rows, wide), BF),
        pltpu.SemaphoreType.DMA((len(blocks), max(counts))),
        pltpu.SemaphoreType.DMA((len(blocks) * (2 if halves else 1),)),
    ]
    return pl.pallas_call(
        functools.partial(pick_kernel, capacity, counts, halves),
        out_shape=out_shape,
        in_specs=[SCALAR] + [ANY] * len(flat),
        out_specs=[ANY, HELD] + [ANY] * (len(out_shape) - 2),
        scratch_shapes=scratch,
        compiler_params=params(scratch, 3),
        cost_estimate=cost(2 * rows * tok_rows * wide, 6 * rows * wide),
        name="pick_rows",
    )(me, *flat)


def expert_kernel(count, capacity, blocks, me, *refs):
    parts, refs = refs[:count], refs[count:]
    pick_count = count if blocks else 0
    picks, refs = refs[:pick_count], refs[pick_count:]
    gate, up, down = refs[:3]
    hidden_far, refs = refs[3:6], refs[6:]
    flat, refs = refs[: 2 * blocks], refs[2 * blocks :]
    gate_out, up_out, weighted_out, rows, sems, out_sems = refs[:6]
    if blocks:
        back, low_dense, high_dense = refs[6:]
    sent = Outgoing(out_sems)
    wait_all(copy_all(stacked(parts, rows), sems))
    width, hidden = gate.shape
    tail, grad_band = pl.ds(width, LANES), pl.ds(width + LANES, width)
    tokens, grads = rows[:, pl.ds(0, width)], rows[:, grad_band]
    lane = lax.broadcasted_iota(jnp.int32, (rows.shape[0], LANES), 1)
    scale = jnp.where(lane == me[0], rows[:, tail].astype(F32), 0.0)
    scale = jnp.sum(scale, axis=1, keepdims=True)
    prob = jnp.zeros((rows.shape[0], 1), F32)
    for low, high in spans_of(hidden):
        pre_gate = product(tokens, gate[:, low:high])
        pre_up = product(tokens, up[:, low:high])
        plain = right_product(grads, down[low:high, :])
        sigma = jax.nn.sigmoid(pre_gate)
        active = pre_gate * sigma
        held = active * pre_up
        if blocks:
            prob += jnp.sum(held.astype(BF).astype(F32) * plain, axis=1, keepdims=True)
        hidden_grad = scale * plain
        slope = pre_up * sigma * (1.0 + pre_gate * (1.0 - sigma))
        gate_out[:, low:high] = (hidden_grad * slope).astype(BF)
        up_out[:, low:high] = (hidden_grad * active).astype(BF)
        weighted_out[:, low:high] = (scale * held).astype(BF)
    for near, far_out in zip((gate_out, up_out, weighted_out), hidden_far):
        sent.send(near, far_out)
    if not blocks:
        sent.wait()
        return
    outs = flat[:blocks], flat[blocks:]
    for low, high in spans_of(width):
        total = right_product(gate_out[...], gate[low:high, :])
        total = total + right_product(up_out[...], up[low:high, :])
        back[:, low:high] = total.astype(BF)
    back[:, width:] = jnp.where(lane == me[0], prob, 0.0).astype(BF)
    half = width // 2
    at, j = 0, 0
    for pick in picks:
        unit = eye(pick.shape[1])
        for first in range(0, pick.shape[0], capacity):
            turned = right_product(unit, pick[pl.ds(first, capacity), :]).astype(BF)
            taken = pl.ds(at + first, capacity)
            bands = ((pl.ds(0, half), low_dense), (pl.ds(half, half + LANES), high_dense))
            for side, (band, dense) in enumerate(bands):
                dense[j] = product(turned, back[taken, band]).astype(BF)
                sent.send(dense.at[j], outs[side][j])
            j += 1
        at += pick.shape[0]
    sent.wait()


def expert_rows(me, capacity, parts, mats, picks=()):
    width, hidden = mats[0].shape
    rows = sum(part.shape[0] for part in parts)
    blocks = rows // capacity if picks else 0
    out_shape = [far_shape(rows, hidden)] * 3
    scratch = [pltpu.VMEM((rows, hidden), BF)] * 3 + [
        pltpu.VMEM((rows, parts[0].shape[1]), BF),
        pltpu.SemaphoreType.DMA((len(parts),)),
        pltpu.SemaphoreType.DMA((3 + 2 * blocks,)),
    ]
    if picks:
        tok_rows = picks[0].shape[1]
        out_shape += [far_shape(tok_rows, width // 2)] * blocks
        out_shape += [far_shape(tok_rows, width // 2 + LANES)] * blocks
        scratch += [
            pltpu.VMEM((rows, width + LANES), BF),
            pltpu.VMEM((blocks, tok_rows, width // 2), BF),
            pltpu.VMEM((blocks, tok_rows, width // 2 + LANES), BF),
        ]
    made = pl.pallas_call(
        functools.partial(expert_kernel, len(parts), capacity, blocks),
        out_shape=out_shape,
        in_specs=[SCALAR] + [ANY] * len(parts) + [HELD] * (len(picks) + 3),
        out_specs=[ANY] * len(out_shape),
        scratch_shapes=scratch,
        compiler_params=params(scratch, 5),
        cost_estimate=cost((10 if picks else 6) * rows * width * hidden, 2 * rows * width),
        name="expert_rows",
    )(me, *parts, *picks, *mats)
    return made[:3], (made[3 : 3 + blocks], made[3 + blocks :])


def add_kernel(count, *refs):
    ins, outs, (held, made, sems, out_sems) = refs[: 2 * count], refs[2 * count : 3 * count], refs[3 * count :]
    copies = copy_all([(part, held.at[i]) for i, part in enumerate(ins)], sems)
    sent = Outgoing(out_sems)
    for side in range(count):
        copies[side].wait()
        copies[count + side].wait()
        made[side] = (held[count + side].astype(F32) + held[side].astype(F32)).astype(BF)
        sent.send(made.at[side], outs[side])
    sent.wait()


def add_blocks(run, terms):
    rows, width = terms[0].shape
    count = len(run)
    scratch = [
        pltpu.VMEM((2 * count, rows, width), BF),
        pltpu.VMEM((count, rows, width), BF),
        pltpu.SemaphoreType.DMA((2 * count,)),
        pltpu.SemaphoreType.DMA((count,)),
    ]
    return pl.pallas_call(
        functools.partial(add_kernel, count),
        out_shape=[far_shape(rows, width)] * count,
        in_specs=[ANY] * (2 * count),
        out_specs=[ANY] * count,
        scratch_shapes=scratch,
        compiler_params=params(scratch, 3),
        cost_estimate=cost(count * rows * width, 6 * count * rows * width),
        name="add_blocks",
    )(*run, *terms)


def finish_kernel(count, routes, *refs):
    lows, highs = refs[:count], refs[count : 2 * count]
    out, prob_out, low_held, high_held, low_sems, high_sems = refs[2 * count :]
    first = copy_all([(part, low_held.at[i]) for i, part in enumerate(lows)], low_sems)
    second = copy_all([(part, high_held.at[i]) for i, part in enumerate(highs)], high_sems)
    half = low_held.shape[2]
    wait_all(first)
    total = low_held[0].astype(F32)
    for i in range(1, count):
        total += low_held[i].astype(F32)
    out[:, :half] = total.astype(BF)
    wait_all(second)
    total = high_held[0].astype(F32)
    for i in range(1, count):
        total += high_held[i].astype(F32)
    out[:, half:] = total[:, :half].astype(BF)
    tail = right_product(eye(LANES), total[:, half:].astype(BF))
    expert = lax.broadcasted_iota(jnp.int32, tail.shape, 0)
    for k in range(routes.shape[0]):
        mine = jnp.where(expert == routes[k : k + 1, :], tail, 0.0)
        prob_out[k : k + 1, :] = jnp.sum(mine, axis=0, keepdims=True).astype(BF)


def finish(routes, lows, highs):
    rows, width = lows[0].shape
    count = len(lows)
    scratch = [
        pltpu.VMEM((count, rows, width), BF),
        pltpu.VMEM((count, rows, width + LANES), BF),
        pltpu.SemaphoreType.DMA((count,)),
        pltpu.SemaphoreType.DMA((count,)),
    ]
    out, prob = pl.pallas_call(
        functools.partial(finish_kernel, count),
        out_shape=(shape_of(rows, 2 * width), shape_of(*routes.T.shape)),
        in_specs=[HELD] + [ANY] * (2 * count),
        scratch_shapes=scratch,
        compiler_params=params(scratch, 3),
        cost_estimate=cost(6 * rows * width, 16 * rows * width),
        name="finish",
    )(routes.T, *lows, *highs)
    return out, prob.T


def share_kernel(across_count, count, offsets, copy, *refs):
    across, tiles, refs = refs[:across_count], refs[across_count : across_count + 3 * count], refs[-9:]
    out, first, second, grads, turned, made, sems, grad_sems, out_sems = refs
    share = first.shape[1]
    near = []
    for i, (offset, columns) in enumerate(zip(offsets, (first, second))):
        low = pl.multiple_of(offset + copy[0] * share, LANES)
        near.append(copy_all(stacked(across, columns, pl.ds(low, share)), sems.at[i]))
    later = []
    for kind in range(3):
        some = tiles[kind * count : (kind + 1) * count]
        later.append(copy_all(stacked(some, grads.at[kind]), grad_sems.at[kind]))
    sent = Outgoing(out_sems)
    for kind in range(3):
        if kind != 1:
            wait_all(near[kind // 2])
            columns = second if kind else first
            turned[...] = right_product(eye(share), columns[...]).astype(BF)
        wait_all(later[kind])
        rows = pl.ds(kind * share, share)
        for low, high in spans_of(grads.shape[2]):
            made[rows, low:high] = product(turned[...], grads[kind, :, low:high]).astype(BF)
        sent.send(made.at[rows, :], out.at[rows, :])
    sent.wait()


def share_products(copy, share, offsets, across, grads):
    rows = sum(part.shape[0] for part in across)
    hidden = grads[0][0].shape[1]
    count = len(grads[0])
    ins = [*across, *[far(part) for kind in grads for part in kind]]
    scratch = [
        pltpu.VMEM((rows, share), BF),
        pltpu.VMEM((rows, share), BF),
        pltpu.VMEM((3, rows, hidden), BF),
        pltpu.VMEM((share, rows), BF),
        pltpu.VMEM((3 * share, hidden), BF),
        pltpu.SemaphoreType.DMA((2, len(across))),
        pltpu.SemaphoreType.DMA((3, count)),
        pltpu.SemaphoreType.DMA((3,)),
    ]
    return pl.pallas_call(
        functools.partial(share_kernel, len(across), count, offsets),
        out_shape=far_shape(3 * share, hidden),
        in_specs=[SCALAR] + [ANY] * len(ins),
        out_specs=ANY,
        scratch_shapes=scratch,
        compiler_params=params(scratch, 4),
        cost_estimate=cost(6 * rows * share * hidden, 6 * rows * hidden),
        name="share_products",
    )(copy, *ins)


def merge_kernel(kept, given, gate_out, up_out, down_out, first, second, made, turned, sems, out_sems):
    share = gate_out.shape[0]
    copies = []
    for kind in range(3):
        rows = pl.ds(kind * share, share)
        pairs = ((kept.at[rows, :], first.at[rows, :]), (given.at[rows, :], second.at[rows, :]))
        copies.append(copy_all(pairs, sems.at[kind]))
    sent = Outgoing(out_sems)
    for kind, out in enumerate((gate_out, up_out, down_out)):
        wait_all(copies[kind])
        rows = pl.ds(kind * share, share)
        made[rows, :] = (first[rows, :].astype(F32) + second[rows, :].astype(F32)).astype(BF)
        if kind < 2:
            sent.send(made.at[rows, :], out)
            continue
        for low, high in spans_of(made.shape[1]):
            turned[low:high, :] = right_product(eye(high - low), made[rows, low:high]).astype(BF)
        sent.send(turned, out)
    sent.wait()


def merge(kept, given):
    rows, hidden = kept.shape
    share = rows // 3
    shapes = ((share, hidden), (share, hidden), (hidden, share))
    scratch = [pltpu.VMEM((rows, hidden), BF)] * 3 + [
        pltpu.VMEM((hidden, share), BF),
        pltpu.SemaphoreType.DMA((3, 2)),
        pltpu.SemaphoreType.DMA((3,)),
    ]
    return pl.pallas_call(
        merge_kernel,
        out_shape=[far_shape(*shape) for shape in shapes],
        in_specs=[ANY, ANY],
        out_specs=[ANY] * 3,
        scratch_shapes=scratch,
        compiler_params=params(scratch, 4),
        cost_estimate=cost(rows * hidden, 6 * rows * hidden),
        name="merge",
    )(far(kept), given)


def body(tokens, grad_out, routes, route_weight, w_gate, w_up, w_down):
    tok_rows, model_width = tokens.shape
    route_count = routes.shape[1]
    experts = lax.axis_size("expert")
    copies = lax.axis_size("dp")
    mirrors = copies // 2
    half_ring = experts // 2
    capacity = 4 * tok_rows * route_count // (3 * experts)
    share = model_width // copies
    mats = load_weights(w_gate[0], w_up[0], w_down[0])
    ring = ring_order(experts)
    ahead = [(ring[i], ring[(i + 1) % experts]) for i in range(experts)]
    behind = [(ring[i], ring[(i - 1) % experts]) for i in range(experts)]
    me = lax.axis_index("expert").astype(jnp.int32).reshape(1)
    copy_here = lax.axis_index("dp").astype(jnp.int32).reshape(1)

    offsets = [0]
    for step in range(1, half_ring):
        offsets += [-step, step]
    offsets.append(half_ring)
    at_offset = {offset: index for index, offset in enumerate(offsets)}

    mirror_maps = [
        [(d, (d + 2 * turn) % copies) for d in range(copies)] for turn in range(1, mirrors)
    ]
    own, others, picks = [], [[] for _ in mirror_maps], []

    def pick_blocks(blocks, *deps, **how):
        rows, pick, *split = pick_rows(me, capacity, after(blocks, *deps), **how)
        picks.append(pick)
        own.append(rows)
        for turn, pairs in enumerate(mirror_maps):
            others[turn].append(lax.ppermute(rows, "dp", pairs))
        return split

    parts, all_rows, dense = [], [], [[], []]

    def mirror_group(group, *deps):
        for taken in others:
            rows = after(taken[group], *deps)
            parts.append(expert_rows(me, capacity, rows, mats)[0])
            all_rows.extend(rows)
        return parts[-1][0]

    def expert_group(group, *deps):
        rows = [far(part) for part in after(own[group], *deps)]
        grown, halves = expert_rows(me, capacity, rows, mats, picks[group])
        parts.append(grown)
        all_rows.extend(rows)
        for side in range(2):
            dense[side] += halves[side]

    packed = pack(tokens, grad_out, routes, route_weight)
    pair = packed, packed
    for step in range(1, half_ring):
        run = lax.ppermute(pair[0], "expert", ahead), lax.ppermute(pair[1], "expert", behind)
        if step == 1:
            pick_blocks([(packed,)])
        else:
            pick_blocks([(block,) for block in pair])
        done = picks[-1]
        if step == 2:
            expert_group(slice(0, 2))
            done = dense[0][0]
        if step == half_ring - 1:
            expert_group(slice(2, step))
            done = mirror_group(slice(0, step - 1), dense[0][-1])
        if step > 1:
            done = done, [taken[step - 2] for taken in others]
        pair = lax.optimization_barrier((run, done))[0]
    split = pick_blocks([(block,) for block in pair], halves=True)
    last = (lax.ppermute(split[0], "expert", ahead), lax.ppermute(split[1], "expert", behind))
    pick_blocks([last], [taken[half_ring - 2] for taken in others])
    expert_group(slice(half_ring - 1, None))

    core_pairs = [(d, d ^ 1) for d in range(copies)]

    def shares(copy, *deps):
        grads = [[part[kind] for part in parts] for kind in range(3)]
        offsets = (0, model_width + LANES)
        return share_products(after(copy, *deps), share, offsets, all_rows, grads)

    far_at = at_offset[half_ring]
    run = [[dense[0][far_at], None], [None, dense[1][far_at]]]
    before = run[1][1]
    for step in range(half_ring - 1, -1, -1):
        for which in range(2):
            for side, pairs in enumerate((ahead, behind)):
                if run[which][side] is not None:
                    run[which][side] = lax.ppermute(run[which][side], "expert", pairs)
        if step == 0:
            break
        if step == half_ring - 1:
            before = (before, mirror_group(slice(step - 1, step), before))
        elif step == half_ring - 2:
            before = (before, mirror_group(slice(half_ring - 1, None), before))
        elif step == half_ring - 3:
            sent_share = shares(copy_here ^ 1, before)
            before = (before, sent_share)
        for which in range(2):
            terms = [dense[which][at_offset[sign * step]] for sign in (1, -1)]
            sides = [side for side in range(2) if run[which][side] is not None]
            sums = add_blocks(
                [after(run[which][side], before) for side in sides], [terms[side] for side in sides]
            )
            for side in range(2):
                run[which][side] = sums[sides.index(side)] if side in sides else terms[side]
            before = sums[0]
    given = lax.ppermute(after(sent_share, before), "dp", core_pairs)
    kept = shares(copy_here, before)
    token_grad, prob_out = finish(
        routes, *[(*after(run[which], kept), dense[which][0]) for which in range(2)]
    )
    wgrads = [part[None] for part in merge(kept, given)]
    return (token_grad, prob_out, *wgrads)


def solution(mesh):
    in_specs = (
        P(("dp", "expert"), None),
        P(("dp", "expert"), None),
        P(("dp", "expert"), None),
        P(("dp", "expert"), None),
        P("expert", None, None),
        P("expert", None, None),
        P("expert", None, None),
    )
    out_specs = (
        P(("dp", "expert"), None),
        P(("dp", "expert"), None),
        P("expert", "dp", None),
        P("expert", "dp", None),
        P("expert", None, "dp"),
    )
    return jax.shard_map(body, mesh=mesh, in_specs=in_specs, out_specs=out_specs, check_vma=False)
```

```python
import functools
import math

import jax
import jax.numpy as jnp
from jax import lax
from jax.experimental import pallas as pl
from jax.experimental.pallas import tpu as pltpu
from jax.sharding import PartitionSpec as P

BF = jnp.bfloat16
F32 = jnp.float32
LANES = 128
TILE = 256
MIB = 1024 * 1024


def ring_order(count):
    inner = 2 if count <= 8 else 4
    outer = count // inner
    cycle = [row * inner for row in range(outer)]
    for row in reversed(range(outer)):
        columns = list(range(1, inner))
        if (outer - 1 - row) % 2:
            columns.reverse()
        cycle += [row * inner + column for column in columns]
    return cycle


def product(left, right):
    return jnp.dot(left, right, preferred_element_type=F32)


def right_product(left, right):
    return lax.dot_general(left, right, (((1,), (1,)), ((), ())), preferred_element_type=F32)


def left_product(left, right):
    return lax.dot_general(left, right, (((0,), (0,)), ((), ())), preferred_element_type=F32)


ANY = pl.BlockSpec(memory_space=pl.ANY)
HELD = pl.BlockSpec(memory_space=pltpu.VMEM)
SCALAR = pl.BlockSpec(memory_space=pltpu.SMEM)


def far_shape(rows, columns):
    return pltpu.HBM((rows, columns), BF)


def shape_of(rows, columns, kind=BF):
    return jax.ShapeDtypeStruct((rows, columns), kind)


def cost(flops, moved):
    return pl.CostEstimate(flops=int(flops), bytes_accessed=int(moved), transcendentals=0)


def params(scratch, spare):
    held = [math.prod(one.shape) * 2 for one in scratch if one.memory_space == pltpu.VMEM]
    return pltpu.CompilerParams(vmem_limit_bytes=sum(held) + spare * MIB)


def far(array):
    return pltpu.with_memory_space_constraint(array, pltpu.HBM)


def after(value, *deps):
    if not deps:
        return value
    return lax.optimization_barrier((value, deps))[0]


def spans_of(width):
    return [(low, min(low + TILE, width)) for low in range(0, width, TILE)]


def copy_all(pairs, sems):
    copies = [pltpu.make_async_copy(a, b, sems.at[i]) for i, (a, b) in enumerate(pairs)]
    for copy in copies:
        copy.start()
    return copies


def wait_all(copies):
    for copy in copies:
        copy.wait()


class Outgoing:
    def __init__(self, sems):
        self.sems, self.copies = sems, []

    def send(self, source, target):
        copy = pltpu.make_async_copy(source, target, self.sems.at[len(self.copies)])
        copy.start()
        self.copies.append(copy)

    def wait(self):
        wait_all(self.copies)


def stacked(parts, into, columns=None):
    pairs, at = [], 0
    for part in parts:
        source = part if columns is None else part.at[:, columns]
        pairs.append((source, into.at[pl.ds(at, part.shape[0]), :]))
        at += part.shape[0]
    return pairs


def eye(size):
    first = lax.broadcasted_iota(jnp.int32, (size, size), 0)
    second = lax.broadcasted_iota(jnp.int32, (size, size), 1)
    return (first == second).astype(F32).astype(BF)


def load_kernel(*refs):
    count = (len(refs) - 1) // 2
    wait_all(copy_all(zip(refs[:count], refs[count : 2 * count]), refs[-1]))


def load_weights(*mats):
    return pl.pallas_call(
        load_kernel,
        out_shape=tuple(pltpu.VMEM(mat.shape, mat.dtype) for mat in mats),
        in_specs=[ANY] * len(mats),
        scratch_shapes=[pltpu.SemaphoreType.DMA((len(mats),))],
        compiler_params=params([], 2),
        cost_estimate=cost(0, 4 * sum(mat.size for mat in mats)),
        name="load_weights",
    )(*[far(mat) for mat in mats])


def pack_kernel(tokens, grads, routes, weights, out, held, turned, sems):
    rows, width = tokens.shape
    pairs = ((tokens, pl.ds(0, width)), (grads, pl.ds(width + LANES, width)))
    copies = copy_all([(part, held.at[:, band]) for part, band in pairs], sems)
    expert = lax.broadcasted_iota(jnp.int32, (LANES, rows), 0)
    dense = jnp.zeros((LANES, rows), F32)
    for k in range(routes.shape[0]):
        dense += jnp.where(routes[k : k + 1, :] == expert, weights[k : k + 1, :].astype(F32), 0.0)
    turned[...] = dense.astype(BF)
    held[:, width : width + LANES] = right_product(eye(rows), turned[...]).astype(BF)
    wait_all(copies)
    wait_all(copy_all([(held, out)], sems))


def pack(tokens, grads, routes, weights):
    rows, width = tokens.shape
    scratch = [
        pltpu.VMEM((rows, 2 * width + LANES), BF),
        pltpu.VMEM((LANES, rows), BF),
        pltpu.SemaphoreType.DMA((2,)),
    ]
    return pl.pallas_call(
        pack_kernel,
        out_shape=far_shape(rows, 2 * width + LANES),
        in_specs=[ANY, ANY, HELD, HELD],
        out_specs=ANY,
        scratch_shapes=scratch,
        compiler_params=params(scratch, 3),
        cost_estimate=cost(1e6, 8 * rows * width),
        name="pack",
    )(far(tokens), far(grads), routes.T, weights.T)


def pick_kernel(capacity, counts, halves, me, *refs):
    total = sum(counts)
    blocks, refs = refs[:total], refs[total:]
    rows_out, choice, refs = refs[0], refs[1], refs[2:]
    split, (held, made, sems, out_sems) = refs[:-4], refs[-4:]
    tok_rows = choice.shape[1]
    width = (held.shape[1] - LANES) // 2
    wide = width + LANES
    copies, at = [], 0
    for j, count in enumerate(counts):
        rows, low, pairs = pl.ds(j * tok_rows, tok_rows), 0, []
        for part in blocks[at : at + count]:
            pairs.append((part, held.at[rows, pl.ds(low, part.shape[1])]))
            low += part.shape[1]
        copies.append(copy_all(pairs, sems.at[j]))
        at += count
    lane = lax.broadcasted_iota(jnp.int32, (8, LANES), 1)
    mine = (lane == me[0]).astype(F32).astype(BF)
    first = lax.broadcasted_iota(jnp.int32, (tok_rows, tok_rows), 0)
    second = lax.broadcasted_iota(jnp.int32, (tok_rows, tok_rows), 1)
    earlier = (first < second).astype(F32).astype(BF)
    want = lax.broadcasted_iota(jnp.int32, (capacity, tok_rows), 0)
    sent = Outgoing(out_sems)
    for j in range(len(counts)):
        wait_all(copies[j])
        near = pl.ds(j * tok_rows, tok_rows)
        if halves:
            band = pl.ds(wide, width) if j else pl.ds(0, wide)
            sent.send(held.at[near, band], split[j])
        out = pl.ds(j * capacity, capacity)
        block = held[near, :]
        routed = right_product(mine, block[:, width:wide]) > 0
        slot = product(routed.astype(F32).astype(BF), earlier)
        slot = jnp.where(routed, slot, -1.0).astype(jnp.int32)
        pick = (want == slot[0:1, :]).astype(F32).astype(BF)
        choice[out, :] = pick
        made[out, :] = product(pick, block).astype(BF)
        sent.send(made.at[out, :], rows_out.at[out, :])
    sent.wait()


def pick_rows(me, capacity, blocks, halves=False):
    counts = [len(parts) for parts in blocks]
    flat = [part for parts in blocks for part in parts]
    wide = sum(part.shape[1] for part in blocks[0])
    tok_rows = flat[0].shape[0]
    rows = capacity * len(blocks)
    width = (wide - LANES) // 2
    out_shape = [far_shape(rows, wide), shape_of(rows, tok_rows)]
    if halves:
        out_shape += [far_shape(tok_rows, width + LANES), far_shape(tok_rows, width)]
    scratch = [
        pltpu.VMEM((tok_rows * len(blocks), wide), BF),
        pltpu.VMEM((rows, wide), BF),
        pltpu.SemaphoreType.DMA((len(blocks), max(counts))),
        pltpu.SemaphoreType.DMA((len(blocks) * (2 if halves else 1),)),
    ]
    return pl.pallas_call(
        functools.partial(pick_kernel, capacity, counts, halves),
        out_shape=out_shape,
        in_specs=[SCALAR] + [ANY] * len(flat),
        out_specs=[ANY, HELD] + [ANY] * (len(out_shape) - 2),
        scratch_shapes=scratch,
        compiler_params=params(scratch, 3),
        cost_estimate=cost(2 * rows * tok_rows * wide, 6 * rows * wide),
        name="pick_rows",
    )(me, *flat)


def expert_kernel(count, capacity, blocks, halves, me, *refs):
    parts, refs = refs[:count], refs[count:]
    pick_count = count if blocks else 0
    picks, refs = refs[:pick_count], refs[pick_count:]
    gate, up, down = refs[:3]
    hidden_far, refs = refs[3:6], refs[6:]
    outs, refs = refs[: blocks + halves], refs[blocks + halves :]
    gate_out, up_out, weighted_out, rows, sems, out_sems = refs[:6]
    if blocks:
        back, dense = refs[6:]
    sent = Outgoing(out_sems)
    wait_all(copy_all(stacked(parts, rows), sems))
    width, hidden = gate.shape
    tail, grad_band = pl.ds(width, LANES), pl.ds(width + LANES, width)
    tokens, grads = rows[:, pl.ds(0, width)], rows[:, grad_band]
    lane = lax.broadcasted_iota(jnp.int32, (rows.shape[0], LANES), 1)
    scale = jnp.where(lane == me[0], rows[:, tail].astype(F32), 0.0)
    scale = jnp.sum(scale, axis=1, keepdims=True)
    prob = jnp.zeros((rows.shape[0], 1), F32)
    for low, high in spans_of(hidden):
        pre_gate = product(tokens, gate[:, low:high])
        pre_up = product(tokens, up[:, low:high])
        plain = right_product(grads, down[low:high, :])
        sigma = jax.nn.sigmoid(pre_gate)
        active = pre_gate * sigma
        held = active * pre_up
        if blocks:
            prob += jnp.sum(held.astype(BF).astype(F32) * plain, axis=1, keepdims=True)
        hidden_grad = scale * plain
        slope = pre_up * sigma * (1.0 + pre_gate * (1.0 - sigma))
        gate_out[:, low:high] = (hidden_grad * slope).astype(BF)
        up_out[:, low:high] = (hidden_grad * active).astype(BF)
        weighted_out[:, low:high] = (scale * held).astype(BF)
    for near, far_out in zip((gate_out, up_out, weighted_out), hidden_far):
        sent.send(near, far_out)
    if not blocks:
        sent.wait()
        return
    for low, high in spans_of(width):
        total = right_product(gate_out[...], gate[low:high, :])
        total = total + right_product(up_out[...], up[low:high, :])
        back[:, low:high] = total.astype(BF)
    back[:, width:] = jnp.where(lane == me[0], prob, 0.0).astype(BF)
    half = width // 2
    at, j = 0, 0
    for pick in picks:
        unit = eye(pick.shape[1])
        for first in range(0, pick.shape[0], capacity):
            turned = right_product(unit, pick[pl.ds(first, capacity), :]).astype(BF)
            dense[j] = product(turned, back[pl.ds(at + first, capacity), :]).astype(BF)
            if halves and j == blocks - 1:
                sent.send(dense.at[j, :, pl.ds(0, half)], outs[j])
                sent.send(dense.at[j, :, pl.ds(half, half + LANES)], outs[j + 1])
            else:
                sent.send(dense.at[j], outs[j])
            j += 1
        at += pick.shape[0]
    sent.wait()


def expert_rows(me, capacity, parts, mats, picks=(), halves=False):
    width, hidden = mats[0].shape
    rows = sum(part.shape[0] for part in parts)
    blocks = rows // capacity if picks else 0
    out_shape = [far_shape(rows, hidden)] * 3
    scratch = [pltpu.VMEM((rows, hidden), BF)] * 3 + [
        pltpu.VMEM((rows, parts[0].shape[1]), BF),
        pltpu.SemaphoreType.DMA((len(parts),)),
        pltpu.SemaphoreType.DMA((4 + blocks,)),
    ]
    if picks:
        tok_rows = picks[0].shape[1]
        out_shape += [far_shape(tok_rows, width + LANES)] * (blocks - halves)
        if halves:
            out_shape += [far_shape(tok_rows, width // 2 + extra) for extra in (0, LANES)]
        scratch += [
            pltpu.VMEM((rows, width + LANES), BF),
            pltpu.VMEM((blocks, tok_rows, width + LANES), BF),
        ]
    made = pl.pallas_call(
        functools.partial(expert_kernel, len(parts), capacity, blocks, halves),
        out_shape=out_shape,
        in_specs=[SCALAR] + [ANY] * len(parts) + [HELD] * (len(picks) + 3),
        out_specs=[ANY] * len(out_shape),
        scratch_shapes=scratch,
        compiler_params=params(scratch, 5),
        cost_estimate=cost((10 if picks else 6) * rows * width * hidden, 2 * rows * width),
        name="expert_rows",
    )(me, *parts, *picks, *mats)
    return made[:3], made[3:]


def add_kernel(ahead, behind, ahead_term, behind_term, *refs):
    ahead_out, behind_out, held, made, sems, out_sems = refs
    width = held.shape[2]
    bands = pl.ds(0, ahead.shape[1]), pl.ds(width - behind.shape[1], behind.shape[1])
    copies = copy_all(
        [
            (ahead, held.at[0, :, bands[0]]),
            (behind, held.at[1, :, bands[1]]),
            (ahead_term, made.at[0]),
            (behind_term, made.at[1]),
        ],
        sems,
    )
    sent = Outgoing(out_sems)
    for side, out in enumerate((ahead_out, behind_out)):
        copies[side].wait()
        copies[2 + side].wait()
        band = bands[side]
        total = made[side, :, band].astype(F32) + held[side, :, band].astype(F32)
        made[side, :, band] = total.astype(BF)
        sent.send(made.at[side], out)
    sent.wait()


def add_blocks(run, terms):
    rows, width = terms[0].shape
    scratch = [
        pltpu.VMEM((2, rows, width), BF),
        pltpu.VMEM((2, rows, width), BF),
        pltpu.SemaphoreType.DMA((4,)),
        pltpu.SemaphoreType.DMA((2,)),
    ]
    return pl.pallas_call(
        add_kernel,
        out_shape=[far_shape(rows, width)] * 2,
        in_specs=[ANY] * 4,
        out_specs=[ANY] * 2,
        scratch_shapes=scratch,
        compiler_params=params(scratch, 3),
        cost_estimate=cost(2 * rows * width, 12 * rows * width),
        name="add_blocks",
    )(*run, *terms)


def finish_kernel(routes, first, second, own, out, prob_out, held, sems):
    copies = copy_all([(part, held.at[i]) for i, part in enumerate((first, second, own))], sems)
    wait_all(copies)
    width = out.shape[1]
    total = held[0].astype(F32) + held[1].astype(F32) + held[2].astype(F32)
    out[...] = total[:, :width].astype(BF)
    tail = right_product(eye(LANES), total[:, width:].astype(BF))
    expert = lax.broadcasted_iota(jnp.int32, tail.shape, 0)
    for k in range(routes.shape[0]):
        mine = jnp.where(expert == routes[k : k + 1, :], tail, 0.0)
        prob_out[k : k + 1, :] = jnp.sum(mine, axis=0, keepdims=True).astype(BF)


def finish(routes, *parts):
    rows, width = parts[0].shape
    scratch = [
        pltpu.VMEM((len(parts), rows, width), BF),
        pltpu.SemaphoreType.DMA((len(parts),)),
    ]
    out, prob = pl.pallas_call(
        finish_kernel,
        out_shape=(shape_of(rows, width - LANES), shape_of(*routes.T.shape)),
        in_specs=[HELD] + [ANY] * len(parts),
        scratch_shapes=scratch,
        compiler_params=params(scratch, 4),
        cost_estimate=cost(3 * rows * width, 8 * rows * width),
        name="finish",
    )(routes.T, *parts)
    return out, prob.T


def share_kernel(across_count, count, offsets, copy, *refs):
    across, tiles, refs = refs[:across_count], refs[across_count : across_count + 3 * count], refs[-9:]
    out, first, second, grads, turned, made, sems, grad_sems, out_sems = refs
    share = first.shape[1]
    near = []
    for i, (offset, columns) in enumerate(zip(offsets, (first, second))):
        low = pl.multiple_of(offset + copy[0] * share, LANES)
        near.append(copy_all(stacked(across, columns, pl.ds(low, share)), sems.at[i]))
    later = []
    for kind in range(3):
        some = tiles[kind * count : (kind + 1) * count]
        later.append(copy_all(stacked(some, grads.at[kind]), grad_sems.at[kind]))
    sent = Outgoing(out_sems)
    for kind in range(3):
        if kind != 1:
            wait_all(near[kind // 2])
            columns = second if kind else first
            turned[...] = right_product(eye(share), columns[...]).astype(BF)
        wait_all(later[kind])
        rows = pl.ds(kind * share, share)
        for low, high in spans_of(grads.shape[2]):
            made[rows, low:high] = product(turned[...], grads[kind, :, low:high]).astype(BF)
        sent.send(made.at[rows, :], out.at[rows, :])
    sent.wait()


def share_products(copy, share, offsets, across, grads):
    rows = sum(part.shape[0] for part in across)
    hidden = grads[0][0].shape[1]
    count = len(grads[0])
    ins = [*across, *[far(part) for kind in grads for part in kind]]
    scratch = [
        pltpu.VMEM((rows, share), BF),
        pltpu.VMEM((rows, share), BF),
        pltpu.VMEM((3, rows, hidden), BF),
        pltpu.VMEM((share, rows), BF),
        pltpu.VMEM((3 * share, hidden), BF),
        pltpu.SemaphoreType.DMA((2, len(across))),
        pltpu.SemaphoreType.DMA((3, count)),
        pltpu.SemaphoreType.DMA((3,)),
    ]
    return pl.pallas_call(
        functools.partial(share_kernel, len(across), count, offsets),
        out_shape=far_shape(3 * share, hidden),
        in_specs=[SCALAR] + [ANY] * len(ins),
        out_specs=ANY,
        scratch_shapes=scratch,
        compiler_params=params(scratch, 4),
        cost_estimate=cost(6 * rows * share * hidden, 6 * rows * hidden),
        name="share_products",
    )(copy, *ins)


def merge_kernel(kept, given, gate_out, up_out, down_out, first, second, made, turned, sems, out_sems):
    share = gate_out.shape[0]
    copies = []
    for kind in range(3):
        rows = pl.ds(kind * share, share)
        pairs = ((kept.at[rows, :], first.at[rows, :]), (given.at[rows, :], second.at[rows, :]))
        copies.append(copy_all(pairs, sems.at[kind]))
    sent = Outgoing(out_sems)
    for kind, out in enumerate((gate_out, up_out, down_out)):
        wait_all(copies[kind])
        rows = pl.ds(kind * share, share)
        made[rows, :] = (first[rows, :].astype(F32) + second[rows, :].astype(F32)).astype(BF)
        if kind < 2:
            sent.send(made.at[rows, :], out)
            continue
        for low, high in spans_of(made.shape[1]):
            turned[low:high, :] = right_product(eye(high - low), made[rows, low:high]).astype(BF)
        sent.send(turned, out)
    sent.wait()


def merge(kept, given):
    rows, hidden = kept.shape
    share = rows // 3
    shapes = ((share, hidden), (share, hidden), (hidden, share))
    scratch = [pltpu.VMEM((rows, hidden), BF)] * 3 + [
        pltpu.VMEM((hidden, share), BF),
        pltpu.SemaphoreType.DMA((3, 2)),
        pltpu.SemaphoreType.DMA((3,)),
    ]
    return pl.pallas_call(
        merge_kernel,
        out_shape=[far_shape(*shape) for shape in shapes],
        in_specs=[ANY, ANY],
        out_specs=[ANY] * 3,
        scratch_shapes=scratch,
        compiler_params=params(scratch, 4),
        cost_estimate=cost(rows * hidden, 6 * rows * hidden),
        name="merge",
    )(far(kept), given)


def body(tokens, grad_out, routes, route_weight, w_gate, w_up, w_down):
    tok_rows, model_width = tokens.shape
    route_count = routes.shape[1]
    experts = lax.axis_size("expert")
    copies = lax.axis_size("dp")
    mirrors = copies // 2
    half_ring = experts // 2
    capacity = 4 * tok_rows * route_count // (3 * experts)
    share = model_width // copies
    mats = load_weights(w_gate[0], w_up[0], w_down[0])
    ring = ring_order(experts)
    ahead = [(ring[i], ring[(i + 1) % experts]) for i in range(experts)]
    behind = [(ring[i], ring[(i - 1) % experts]) for i in range(experts)]
    me = lax.axis_index("expert").astype(jnp.int32).reshape(1)
    copy_here = lax.axis_index("dp").astype(jnp.int32).reshape(1)

    offsets = [0]
    for step in range(1, half_ring):
        offsets += [-step, step]
    offsets.append(half_ring)
    at_offset = {offset: index for index, offset in enumerate(offsets)}

    mirror_maps = [
        [(d, (d + 2 * turn) % copies) for d in range(copies)] for turn in range(1, mirrors)
    ]
    own, others, picks = [], [[] for _ in mirror_maps], []

    def pick_blocks(blocks, *deps, **how):
        rows, pick, *split = pick_rows(me, capacity, after(blocks, *deps), **how)
        picks.append(pick)
        own.append(rows)
        for turn, pairs in enumerate(mirror_maps):
            others[turn].append(lax.ppermute(rows, "dp", pairs))
        return split

    parts, all_rows, dense = [], [], []

    def mirror_group(group, *deps):
        for taken in others:
            rows = after(taken[group], *deps)
            parts.append(expert_rows(me, capacity, rows, mats)[0])
            all_rows.extend(rows)
        return parts[-1][0]

    def expert_group(group, *deps):
        rows = [far(part) for part in after(own[group], *deps)]
        grown, back = expert_rows(me, capacity, rows, mats, picks[group], group.stop is None)
        parts.append(grown)
        all_rows.extend(rows)
        dense.extend(back)

    packed = pack(tokens, grad_out, routes, route_weight)
    pair = packed, packed
    for step in range(1, half_ring):
        run = lax.ppermute(pair[0], "expert", ahead), lax.ppermute(pair[1], "expert", behind)
        if step == 1:
            pick_blocks([(packed,)])
        else:
            pick_blocks([(block,) for block in pair])
        done = picks[-1]
        if step == 2:
            expert_group(slice(0, 2))
            done = dense[0]
        if step == half_ring - 1:
            expert_group(slice(2, step))
            done = mirror_group(slice(0, step - 1), dense[-1])
        if step > 1:
            done = done, [taken[step - 2] for taken in others]
        pair = lax.optimization_barrier((run, done))[0]
    split = pick_blocks([(block,) for block in pair], halves=True)
    last = (lax.ppermute(split[0], "expert", ahead), lax.ppermute(split[1], "expert", behind))
    pick_blocks([last], [taken[half_ring - 2] for taken in others])
    expert_group(slice(half_ring - 1, None))

    core_pairs = [(d, d ^ 1) for d in range(copies)]

    def shares(copy, *deps):
        grads = [[part[kind] for part in parts] for kind in range(3)]
        offsets = (0, model_width + LANES)
        return share_products(after(copy, *deps), share, offsets, all_rows, grads)

    run = dense[-2:]
    before = run[0]
    for step in range(half_ring - 1, -1, -1):
        run = lax.ppermute(run[0], "expert", ahead), lax.ppermute(run[1], "expert", behind)
        if step == 0:
            break
        if step == half_ring - 1:
            before = before, mirror_group(slice(step - 1, step), before)
        elif step == half_ring - 2:
            before = before, mirror_group(slice(half_ring - 1, None), before)
        elif step == half_ring - 3:
            sent_share = shares(copy_here ^ 1, before)
            before = before, sent_share
        run = add_blocks(after(run, before), [dense[at_offset[sign * step]] for sign in (1, -1)])
        before = run[0]
    given = lax.ppermute(after(sent_share, before), "dp", core_pairs)
    kept = shares(copy_here, before)
    merged = merge(kept, given)
    token_grad, prob_out = finish(routes, *after(run, merged[0]), dense[0])
    wgrads = [part[None] for part in merged]
    return (token_grad, prob_out, *wgrads)


def solution(mesh):
    in_specs = (
        P(("dp", "expert"), None),
        P(("dp", "expert"), None),
        P(("dp", "expert"), None),
        P(("dp", "expert"), None),
        P("expert", None, None),
        P("expert", None, None),
        P("expert", None, None),
    )
    out_specs = (
        P(("dp", "expert"), None),
        P(("dp", "expert"), None),
        P("expert", "dp", None),
        P("expert", "dp", None),
        P("expert", None, "dp"),
    )
    return jax.shard_map(body, mesh=mesh, in_specs=in_specs, out_specs=out_specs, check_vma=False)
```

```python
import functools
import math

import jax
import jax.numpy as jnp
from jax import lax
from jax.experimental import pallas as pl
from jax.experimental.pallas import tpu as pltpu
from jax.sharding import PartitionSpec as P

BF = jnp.bfloat16
F32 = jnp.float32
LANES = 128
TILE = 256
MIB = 1024 * 1024


def ring_order(count):
    inner = 2 if count <= 8 else 4
    outer = count // inner
    cycle = [row * inner for row in range(outer)]
    for row in reversed(range(outer)):
        columns = list(range(1, inner))
        if (outer - 1 - row) % 2:
            columns.reverse()
        cycle += [row * inner + column for column in columns]
    return cycle


def product(left, right):
    return jnp.dot(left, right, preferred_element_type=F32)


def right_product(left, right):
    return lax.dot_general(left, right, (((1,), (1,)), ((), ())), preferred_element_type=F32)


def left_product(left, right):
    return lax.dot_general(left, right, (((0,), (0,)), ((), ())), preferred_element_type=F32)


ANY = pl.BlockSpec(memory_space=pl.ANY)
HELD = pl.BlockSpec(memory_space=pltpu.VMEM)
SCALAR = pl.BlockSpec(memory_space=pltpu.SMEM)


def far_shape(rows, columns):
    return pltpu.HBM((rows, columns), BF)


def shape_of(rows, columns, kind=BF):
    return jax.ShapeDtypeStruct((rows, columns), kind)


def cost(flops, moved):
    return pl.CostEstimate(flops=int(flops), bytes_accessed=int(moved), transcendentals=0)


def params(scratch, spare):
    held = [math.prod(one.shape) * 2 for one in scratch if one.memory_space == pltpu.VMEM]
    return pltpu.CompilerParams(vmem_limit_bytes=sum(held) + spare * MIB)


def far(array):
    return pltpu.with_memory_space_constraint(array, pltpu.HBM)


def after(value, *deps):
    if not deps:
        return value
    return lax.optimization_barrier((value, deps))[0]


def spans_of(width):
    return [(low, min(low + TILE, width)) for low in range(0, width, TILE)]


def copy_all(pairs, sems):
    copies = [pltpu.make_async_copy(a, b, sems.at[i]) for i, (a, b) in enumerate(pairs)]
    for copy in copies:
        copy.start()
    return copies


def wait_all(copies):
    for copy in copies:
        copy.wait()


class Outgoing:
    def __init__(self, sems):
        self.sems, self.copies = sems, []

    def send(self, source, target):
        copy = pltpu.make_async_copy(source, target, self.sems.at[len(self.copies)])
        copy.start()
        self.copies.append(copy)

    def wait(self):
        wait_all(self.copies)


def stacked(parts, into, columns=None):
    pairs, at = [], 0
    for part in parts:
        source = part if columns is None else part.at[:, columns]
        pairs.append((source, into.at[pl.ds(at, part.shape[0]), :]))
        at += part.shape[0]
    return pairs


def eye(size):
    first = lax.broadcasted_iota(jnp.int32, (size, size), 0)
    second = lax.broadcasted_iota(jnp.int32, (size, size), 1)
    return (first == second).astype(F32).astype(BF)


def load_kernel(*refs):
    count = len(refs) // 2 - 1
    wait_all(copy_all(zip(refs[:count], refs[count : 2 * count]), refs[-1]))
    refs[-2][...] = jnp.zeros_like(refs[-2])


def load_weights(*mats):
    return pl.pallas_call(
        load_kernel,
        out_shape=(*[pltpu.VMEM(mat.shape, mat.dtype) for mat in mats], shape_of(8, LANES, F32)),
        in_specs=[ANY] * len(mats),
        scratch_shapes=[pltpu.SemaphoreType.DMA((len(mats),))],
        compiler_params=params([], 2),
        cost_estimate=cost(0, 4 * sum(mat.size for mat in mats)),
        name="load_weights",
    )(*[far(mat) for mat in mats])


def pack_kernel(tokens, grads, far_routes, weights, out, held, turned, routes, sems):
    rows, width = tokens.shape
    pairs = ((tokens, pl.ds(0, width)), (grads, pl.ds(width + LANES, width)))
    pairs = [(part, held.at[:, band]) for part, band in pairs]
    copies = copy_all([(far_routes, routes), *pairs], sems)
    copies[0].wait()
    expert = lax.broadcasted_iota(jnp.int32, (LANES, rows), 0)
    dense = jnp.zeros((LANES, rows), F32)
    for k in range(routes.shape[0]):
        dense += jnp.where(routes[k : k + 1, :] == expert, weights[k : k + 1, :].astype(F32), 0.0)
    turned[...] = dense.astype(BF)
    held[:, width : width + LANES] = right_product(eye(rows), turned[...]).astype(BF)
    wait_all(copies[1:])
    wait_all(copy_all([(held, out)], sems))


def pack(tokens, grads, routes, weights):
    rows, width = tokens.shape
    scratch = [
        pltpu.VMEM((rows, 2 * width + LANES), BF),
        pltpu.VMEM((LANES, rows), BF),
        pltpu.VMEM(routes.T.shape, jnp.int32),
        pltpu.SemaphoreType.DMA((3,)),
    ]
    return pl.pallas_call(
        pack_kernel,
        out_shape=far_shape(rows, 2 * width + LANES),
        in_specs=[ANY, ANY, ANY, HELD],
        out_specs=ANY,
        scratch_shapes=scratch,
        compiler_params=params(scratch, 3),
        cost_estimate=cost(1e6, 8 * rows * width),
        name="pack",
    )(far(tokens), far(grads), far(routes.T), weights.T)


def pick_kernel(capacity, counts, halves, skipped, me, *refs):
    total = sum(counts)
    blocks, refs = refs[:total], refs[total + skipped :]
    rows_out, choice, refs = refs[0], refs[1], refs[2:]
    split, (held, made, sems, out_sems) = refs[:-4], refs[-4:]
    tok_rows = choice.shape[1]
    width = (held.shape[1] - LANES) // 2
    wide = width + LANES
    copies, at = [], 0
    for j, count in enumerate(counts):
        rows, low, pairs = pl.ds(j * tok_rows, tok_rows), 0, []
        for part in blocks[at : at + count]:
            pairs.append((part, held.at[rows, pl.ds(low, part.shape[1])]))
            low += part.shape[1]
        copies.append(copy_all(pairs, sems.at[j]))
        at += count
    lane = lax.broadcasted_iota(jnp.int32, (8, LANES), 1)
    mine = (lane == me[0]).astype(F32).astype(BF)
    first = lax.broadcasted_iota(jnp.int32, (tok_rows, tok_rows), 0)
    second = lax.broadcasted_iota(jnp.int32, (tok_rows, tok_rows), 1)
    earlier = (first < second).astype(F32).astype(BF)
    want = lax.broadcasted_iota(jnp.int32, (capacity, tok_rows), 0)
    sent = Outgoing(out_sems)
    for j in range(len(counts)):
        wait_all(copies[j])
        near = pl.ds(j * tok_rows, tok_rows)
        if halves:
            band = pl.ds(wide, width) if j else pl.ds(0, wide)
            sent.send(held.at[near, band], split[j])
        out = pl.ds(j * capacity, capacity)
        block = held[near, :]
        routed = right_product(mine, block[:, width:wide]) > 0
        slot = product(routed.astype(F32).astype(BF), earlier)
        slot = jnp.where(routed, slot, -1.0).astype(jnp.int32)
        pick = (want == slot[0:1, :]).astype(F32).astype(BF)
        choice[out, :] = pick
        made[out, :] = product(pick, block).astype(BF)
        sent.send(made.at[out, :], rows_out.at[out, :])
    sent.wait()


def pick_rows(me, capacity, blocks, halves=False, behind_of=()):
    counts = [len(parts) for parts in blocks]
    flat = [part for parts in blocks for part in parts]
    wide = sum(part.shape[1] for part in blocks[0])
    tok_rows = flat[0].shape[0]
    rows = capacity * len(blocks)
    width = (wide - LANES) // 2
    out_shape = [far_shape(rows, wide), shape_of(rows, tok_rows)]
    if halves:
        out_shape += [far_shape(tok_rows, width + LANES), far_shape(tok_rows, width)]
    scratch = [
        pltpu.VMEM((tok_rows * len(blocks), wide), BF),
        pltpu.VMEM((rows, wide), BF),
        pltpu.SemaphoreType.DMA((len(blocks), max(counts))),
        pltpu.SemaphoreType.DMA((len(blocks) * (2 if halves else 1),)),
    ]
    return pl.pallas_call(
        functools.partial(pick_kernel, capacity, counts, halves, len(behind_of)),
        out_shape=out_shape,
        in_specs=[SCALAR] + [ANY] * (len(flat) + len(behind_of)),
        out_specs=[ANY, HELD] + [ANY] * (len(out_shape) - 2),
        scratch_shapes=scratch,
        compiler_params=params(scratch, 3),
        cost_estimate=cost(2 * rows * tok_rows * wide, 6 * rows * wide),
        name="pick_rows",
    )(me, *flat, *behind_of)


def expert_kernel(count, capacity, blocks, halves, me, *refs):
    parts, refs = refs[:count], refs[count:]
    pick_count = count if blocks else 0
    picks, refs = refs[:pick_count], refs[pick_count:]
    gate, up, down = refs[:3]
    hidden_far, refs = refs[3:6], refs[6:]
    outs, refs = refs[: blocks + halves], refs[blocks + halves :]
    gate_out, up_out, weighted_out, rows, sems, out_sems = refs[:6]
    if blocks:
        back, dense = refs[6:]
    sent = Outgoing(out_sems)
    wait_all(copy_all(stacked(parts, rows), sems))
    width, hidden = gate.shape
    tail, grad_band = pl.ds(width, LANES), pl.ds(width + LANES, width)
    tokens, grads = rows[:, pl.ds(0, width)], rows[:, grad_band]
    lane = lax.broadcasted_iota(jnp.int32, (rows.shape[0], LANES), 1)
    scale = jnp.where(lane == me[0], rows[:, tail].astype(F32), 0.0)
    scale = jnp.sum(scale, axis=1, keepdims=True)
    prob = jnp.zeros((rows.shape[0], 1), F32)
    for low, high in spans_of(hidden):
        pre_gate = product(tokens, gate[:, low:high])
        pre_up = product(tokens, up[:, low:high])
        plain = right_product(grads, down[low:high, :])
        sigma = jax.nn.sigmoid(pre_gate)
        active = pre_gate * sigma
        held = active * pre_up
        if blocks:
            prob += jnp.sum(held.astype(BF).astype(F32) * plain, axis=1, keepdims=True)
        hidden_grad = scale * plain
        slope = pre_up * sigma * (1.0 + pre_gate * (1.0 - sigma))
        gate_out[:, low:high] = (hidden_grad * slope).astype(BF)
        up_out[:, low:high] = (hidden_grad * active).astype(BF)
        weighted_out[:, low:high] = (scale * held).astype(BF)
    for near, far_out in zip((gate_out, up_out, weighted_out), hidden_far):
        sent.send(near, far_out)
    if not blocks:
        sent.wait()
        return
    for low, high in spans_of(width):
        total = right_product(gate_out[...], gate[low:high, :])
        total = total + right_product(up_out[...], up[low:high, :])
        back[:, low:high] = total.astype(BF)
    back[:, width:] = jnp.where(lane == me[0], prob, 0.0).astype(BF)
    half = width // 2
    at, j = 0, 0
    for pick in picks:
        unit = eye(pick.shape[1])
        for first in range(0, pick.shape[0], capacity):
            turned = right_product(unit, pick[pl.ds(first, capacity), :]).astype(BF)
            dense[j] = product(turned, back[pl.ds(at + first, capacity), :]).astype(BF)
            if halves and j == blocks - 1:
                sent.send(dense.at[j, :, pl.ds(0, half)], outs[j])
                sent.send(dense.at[j, :, pl.ds(half, half + LANES)], outs[j + 1])
            else:
                sent.send(dense.at[j], outs[j])
            j += 1
        at += pick.shape[0]
    sent.wait()


def expert_rows(me, capacity, parts, mats, picks=(), halves=False):
    width, hidden = mats[0].shape
    rows = sum(part.shape[0] for part in parts)
    blocks = rows // capacity if picks else 0
    out_shape = [far_shape(rows, hidden)] * 3
    scratch = [pltpu.VMEM((rows, hidden), BF)] * 3 + [
        pltpu.VMEM((rows, parts[0].shape[1]), BF),
        pltpu.SemaphoreType.DMA((len(parts),)),
        pltpu.SemaphoreType.DMA((4 + blocks,)),
    ]
    if picks:
        tok_rows = picks[0].shape[1]
        out_shape += [far_shape(tok_rows, width + LANES)] * (blocks - halves)
        if halves:
            out_shape += [far_shape(tok_rows, width // 2 + extra) for extra in (0, LANES)]
        scratch += [
            pltpu.VMEM((rows, width + LANES), BF),
            pltpu.VMEM((blocks, tok_rows, width + LANES), BF),
        ]
    made = pl.pallas_call(
        functools.partial(expert_kernel, len(parts), capacity, blocks, halves),
        out_shape=out_shape,
        in_specs=[SCALAR] + [ANY] * len(parts) + [HELD] * (len(picks) + 3),
        out_specs=[ANY] * len(out_shape),
        scratch_shapes=scratch,
        compiler_params=params(scratch, 5),
        cost_estimate=cost((10 if picks else 6) * rows * width * hidden, 2 * rows * width),
        name="expert_rows",
    )(me, *parts, *picks, *mats)
    return made[:3], made[3:]


def add_kernel(ahead, behind, ahead_term, behind_term, *refs):
    ahead_out, behind_out, held, made, sems, out_sems = refs
    width = held.shape[2]
    bands = pl.ds(0, ahead.shape[1]), pl.ds(width - behind.shape[1], behind.shape[1])
    copies = copy_all(
        [
            (ahead, held.at[0, :, bands[0]]),
            (behind, held.at[1, :, bands[1]]),
            (ahead_term, made.at[0]),
            (behind_term, made.at[1]),
        ],
        sems,
    )
    sent = Outgoing(out_sems)
    for side, out in enumerate((ahead_out, behind_out)):
        copies[side].wait()
        copies[2 + side].wait()
        band = bands[side]
        total = made[side, :, band].astype(F32) + held[side, :, band].astype(F32)
        made[side, :, band] = total.astype(BF)
        sent.send(made.at[side], out)
    sent.wait()


def add_blocks(run, terms):
    rows, width = terms[0].shape
    scratch = [
        pltpu.VMEM((2, rows, width), BF),
        pltpu.VMEM((2, rows, width), BF),
        pltpu.SemaphoreType.DMA((4,)),
        pltpu.SemaphoreType.DMA((2,)),
    ]
    return pl.pallas_call(
        add_kernel,
        out_shape=[far_shape(rows, width)] * 2,
        in_specs=[ANY] * 4,
        out_specs=[ANY] * 2,
        scratch_shapes=scratch,
        compiler_params=params(scratch, 3),
        cost_estimate=cost(2 * rows * width, 12 * rows * width),
        name="add_blocks",
    )(*run, *terms)


def finish_kernel(routes, first, second, own, out, prob_out, held, sems):
    copies = copy_all([(part, held.at[i]) for i, part in enumerate((first, second, own))], sems)
    wait_all(copies)
    width = out.shape[1]
    total = held[0].astype(F32) + held[1].astype(F32) + held[2].astype(F32)
    out[...] = total[:, :width].astype(BF)
    tail = right_product(eye(LANES), total[:, width:].astype(BF))
    expert = lax.broadcasted_iota(jnp.int32, tail.shape, 0)
    for k in range(routes.shape[0]):
        mine = jnp.where(expert == routes[k : k + 1, :], tail, 0.0)
        prob_out[k : k + 1, :] = jnp.sum(mine, axis=0, keepdims=True).astype(BF)


def finish(routes, *parts):
    rows, width = parts[0].shape
    scratch = [
        pltpu.VMEM((len(parts), rows, width), BF),
        pltpu.SemaphoreType.DMA((len(parts),)),
    ]
    out, prob = pl.pallas_call(
        finish_kernel,
        out_shape=(shape_of(rows, width - LANES), shape_of(*routes.T.shape)),
        in_specs=[HELD] + [ANY] * len(parts),
        scratch_shapes=scratch,
        compiler_params=params(scratch, 4),
        cost_estimate=cost(3 * rows * width, 8 * rows * width),
        name="finish",
    )(routes.T, *parts)
    return out, prob.T


def share_kernel(across_count, count, offsets, copy, *refs):
    across, tiles, refs = refs[:across_count], refs[across_count : across_count + 3 * count], refs[-9:]
    out, first, second, grads, turned, made, sems, grad_sems, out_sems = refs
    share = first.shape[1]
    near = []
    for i, (offset, columns) in enumerate(zip(offsets, (first, second))):
        low = pl.multiple_of(offset + copy[0] * share, LANES)
        near.append(copy_all(stacked(across, columns, pl.ds(low, share)), sems.at[i]))
    later = []
    for kind in range(3):
        some = tiles[kind * count : (kind + 1) * count]
        later.append(copy_all(stacked(some, grads.at[kind]), grad_sems.at[kind]))
    sent = Outgoing(out_sems)
    for kind in range(3):
        if kind != 1:
            wait_all(near[kind // 2])
            columns = second if kind else first
            turned[...] = right_product(eye(share), columns[...]).astype(BF)
        wait_all(later[kind])
        rows = pl.ds(kind * share, share)
        for low, high in spans_of(grads.shape[2]):
            made[rows, low:high] = product(turned[...], grads[kind, :, low:high]).astype(BF)
        sent.send(made.at[rows, :], out.at[rows, :])
    sent.wait()


def share_products(copy, share, offsets, across, grads):
    rows = sum(part.shape[0] for part in across)
    hidden = grads[0][0].shape[1]
    count = len(grads[0])
    ins = [far(part) for part in (*across, *[part for kind in grads for part in kind])]
    scratch = [
        pltpu.VMEM((rows, share), BF),
        pltpu.VMEM((rows, share), BF),
        pltpu.VMEM((3, rows, hidden), BF),
        pltpu.VMEM((share, rows), BF),
        pltpu.VMEM((3 * share, hidden), BF),
        pltpu.SemaphoreType.DMA((2, len(across))),
        pltpu.SemaphoreType.DMA((3, count)),
        pltpu.SemaphoreType.DMA((3,)),
    ]
    return pl.pallas_call(
        functools.partial(share_kernel, len(across), count, offsets),
        out_shape=far_shape(3 * share, hidden),
        in_specs=[SCALAR] + [ANY] * len(ins),
        out_specs=ANY,
        scratch_shapes=scratch,
        compiler_params=params(scratch, 4),
        cost_estimate=cost(6 * rows * share * hidden, 6 * rows * hidden),
        name="share_products",
    )(copy, *ins)


def merge_kernel(kept, given, gate_out, up_out, down_out, first, second, made, turned, sems, out_sems):
    share = gate_out.shape[0]
    copies = []
    for kind in range(3):
        rows = pl.ds(kind * share, share)
        pairs = ((kept.at[rows, :], first.at[rows, :]), (given.at[rows, :], second.at[rows, :]))
        copies.append(copy_all(pairs, sems.at[kind]))
    sent = Outgoing(out_sems)
    for kind, out in enumerate((gate_out, up_out, down_out)):
        wait_all(copies[kind])
        rows = pl.ds(kind * share, share)
        made[rows, :] = (first[rows, :].astype(F32) + second[rows, :].astype(F32)).astype(BF)
        if kind < 2:
            sent.send(made.at[rows, :], out)
            continue
        for low, high in spans_of(made.shape[1]):
            turned[low:high, :] = right_product(eye(high - low), made[rows, low:high]).astype(BF)
        sent.send(turned, out)
    sent.wait()


def merge(kept, given):
    rows, hidden = kept.shape
    share = rows // 3
    shapes = ((share, hidden), (share, hidden), (hidden, share))
    scratch = [pltpu.VMEM((rows, hidden), BF)] * 3 + [
        pltpu.VMEM((hidden, share), BF),
        pltpu.SemaphoreType.DMA((3, 2)),
        pltpu.SemaphoreType.DMA((3,)),
    ]
    return pl.pallas_call(
        merge_kernel,
        out_shape=[far_shape(*shape) for shape in shapes],
        in_specs=[ANY, ANY],
        out_specs=[ANY] * 3,
        scratch_shapes=scratch,
        compiler_params=params(scratch, 4),
        cost_estimate=cost(rows * hidden, 6 * rows * hidden),
        name="merge",
    )(far(kept), given)


def body(tokens, grad_out, routes, route_weight, w_gate, w_up, w_down):
    tok_rows, model_width = tokens.shape
    route_count = routes.shape[1]
    experts = lax.axis_size("expert")
    copies = lax.axis_size("dp")
    mirrors = copies // 2
    half_ring = experts // 2
    capacity = 4 * tok_rows * route_count // (3 * experts)
    share = model_width // copies
    *mats, loaded = load_weights(w_gate[0], w_up[0], w_down[0])
    ring = ring_order(experts)
    ahead = [(ring[i], ring[(i + 1) % experts]) for i in range(experts)]
    behind = [(ring[i], ring[(i - 1) % experts]) for i in range(experts)]
    me = lax.axis_index("expert").astype(jnp.int32).reshape(1)
    copy_here = lax.axis_index("dp").astype(jnp.int32).reshape(1)

    offsets = [0]
    for step in range(1, half_ring):
        offsets += [-step, step]
    offsets.append(half_ring)
    at_offset = {offset: index for index, offset in enumerate(offsets)}

    mirror_maps = [
        [(d, (d + 2 * turn) % copies) for d in range(copies)] for turn in range(1, mirrors)
    ]
    own, others, picks = [], [[] for _ in mirror_maps], []

    def pick_blocks(blocks, *deps, **how):
        rows, pick, *split = pick_rows(me, capacity, after(blocks, *deps), **how)
        picks.append(pick)
        own.append(rows)
        for turn, pairs in enumerate(mirror_maps):
            others[turn].append(lax.ppermute(rows, "dp", pairs))
        return split

    parts, all_rows, dense = [], [], []

    def mirror_group(group, *deps):
        for taken in others:
            rows = after(taken[group], *deps)
            parts.append(expert_rows(me, capacity, rows, mats)[0])
            all_rows.extend(rows)
        return parts[-1][0]

    def expert_group(group, *deps):
        rows = [far(part) for part in after(own[group], *deps)]
        grown, back = expert_rows(me, capacity, rows, mats, picks[group], group.stop is None)
        parts.append(grown)
        all_rows.extend(rows)
        dense.extend(back)

    packed = pack(tokens, grad_out, routes, route_weight)
    pair = packed, packed
    for step in range(1, half_ring):
        run = lax.ppermute(pair[0], "expert", ahead), lax.ppermute(pair[1], "expert", behind)
        if step == 1:
            pick_blocks([(packed,)], behind_of=(loaded,))
        else:
            pick_blocks([(block,) for block in pair])
        done = picks[-1]
        if step == 2:
            expert_group(slice(0, 2))
            done = dense[0]
        if step == half_ring - 1:
            expert_group(slice(2, step))
            done = mirror_group(slice(0, step - 1), dense[-1])
        if step > 1:
            done = done, [taken[step - 2] for taken in others]
        pair = lax.optimization_barrier((run, done))[0]
    split = pick_blocks([(block,) for block in pair], halves=True)
    last = (lax.ppermute(split[0], "expert", ahead), lax.ppermute(split[1], "expert", behind))
    expert_group(slice(half_ring - 1, half_ring))
    pick_blocks([last], dense[-1])
    expert_group(slice(half_ring, None))

    core_pairs = [(d, d ^ 1) for d in range(copies)]

    def shares(copy, *deps):
        grads = [[part[kind] for part in parts] for kind in range(3)]
        offsets = (0, model_width + LANES)
        return share_products(after(copy, *deps), share, offsets, all_rows, grads)

    run = dense[-2:]
    before = run[0]
    for step in range(half_ring - 1, -1, -1):
        run = lax.ppermute(run[0], "expert", ahead), lax.ppermute(run[1], "expert", behind)
        if step == 0:
            break
        if step == half_ring - 1:
            before = before, mirror_group(slice(step - 1, step), before)
        elif step == half_ring - 2:
            before = before, mirror_group(slice(half_ring - 1, None), before)
        elif step == half_ring - 3:
            sent_share = shares(copy_here ^ 1, before)
            before = before, sent_share
        run = add_blocks(after(run, before), [dense[at_offset[sign * step]] for sign in (1, -1)])
        before = run[0]
    given = lax.ppermute(after(sent_share, before), "dp", core_pairs)
    kept = shares(copy_here, before)
    merged = merge(kept, given)
    token_grad, prob_out = finish(routes, *after(run, merged[0]), dense[0])
    wgrads = [part[None] for part in merged]
    return (token_grad, prob_out, *wgrads)


def solution(mesh):
    in_specs = (
        P(("dp", "expert"), None),
        P(("dp", "expert"), None),
        P(("dp", "expert"), None),
        P(("dp", "expert"), None),
        P("expert", None, None),
        P("expert", None, None),
        P("expert", None, None),
    )
    out_specs = (
        P(("dp", "expert"), None),
        P(("dp", "expert"), None),
        P("expert", "dp", None),
        P("expert", "dp", None),
        P("expert", None, "dp"),
    )
    return jax.shard_map(body, mesh=mesh, in_specs=in_specs, out_specs=out_specs, check_vma=False)
```

```python
import functools
import math

import jax
import jax.numpy as jnp
from jax import lax
from jax.experimental import pallas as pl
from jax.experimental.pallas import tpu as pltpu
from jax.sharding import PartitionSpec as P

BF = jnp.bfloat16
F32 = jnp.float32
LANES = 128
TILE = 256
MIB = 1024 * 1024


def ring_order(count):
    inner = 2 if count <= 8 else 4
    outer = count // inner
    cycle = [row * inner for row in range(outer)]
    for row in reversed(range(outer)):
        columns = list(range(1, inner))
        if (outer - 1 - row) % 2:
            columns.reverse()
        cycle += [row * inner + column for column in columns]
    return cycle


def product(left, right):
    return jnp.dot(left, right, preferred_element_type=F32)


def right_product(left, right):
    return lax.dot_general(left, right, (((1,), (1,)), ((), ())), preferred_element_type=F32)


def left_product(left, right):
    return lax.dot_general(left, right, (((0,), (0,)), ((), ())), preferred_element_type=F32)


ANY = pl.BlockSpec(memory_space=pl.ANY)
HELD = pl.BlockSpec(memory_space=pltpu.VMEM)
SCALAR = pl.BlockSpec(memory_space=pltpu.SMEM)


def far_shape(rows, columns):
    return pltpu.HBM((rows, columns), BF)


def shape_of(rows, columns, kind=BF):
    return jax.ShapeDtypeStruct((rows, columns), kind)


def cost(flops, moved):
    return pl.CostEstimate(flops=int(flops), bytes_accessed=int(moved), transcendentals=0)


def params(scratch, spare):
    held = [math.prod(one.shape) * 2 for one in scratch if one.memory_space == pltpu.VMEM]
    return pltpu.CompilerParams(vmem_limit_bytes=sum(held) + spare * MIB)


def far(array):
    return pltpu.with_memory_space_constraint(array, pltpu.HBM)


def after(value, *deps):
    if not deps:
        return value
    return lax.optimization_barrier((value, deps))[0]


def spans_of(width):
    return [(low, min(low + TILE, width)) for low in range(0, width, TILE)]


def copy_all(pairs, sems):
    copies = [pltpu.make_async_copy(a, b, sems.at[i]) for i, (a, b) in enumerate(pairs)]
    for copy in copies:
        copy.start()
    return copies


def wait_all(copies):
    for copy in copies:
        copy.wait()


class Outgoing:
    def __init__(self, sems):
        self.sems, self.copies = sems, []

    def send(self, source, target):
        copy = pltpu.make_async_copy(source, target, self.sems.at[len(self.copies)])
        copy.start()
        self.copies.append(copy)

    def wait(self):
        wait_all(self.copies)


def stacked(parts, into, columns=None):
    pairs, at = [], 0
    for part in parts:
        source = part if columns is None else part.at[:, columns]
        pairs.append((source, into.at[pl.ds(at, part.shape[0]), :]))
        at += part.shape[0]
    return pairs


def eye(size):
    first = lax.broadcasted_iota(jnp.int32, (size, size), 0)
    second = lax.broadcasted_iota(jnp.int32, (size, size), 1)
    return (first == second).astype(F32).astype(BF)


def load_kernel(*refs):
    count = len(refs) // 2 - 1
    wait_all(copy_all(zip(refs[:count], refs[count : 2 * count]), refs[-1]))
    refs[-2][...] = jnp.zeros_like(refs[-2])


def load_weights(*mats):
    return pl.pallas_call(
        load_kernel,
        out_shape=(*[pltpu.VMEM(mat.shape, mat.dtype) for mat in mats], shape_of(8, LANES, F32)),
        in_specs=[ANY] * len(mats),
        scratch_shapes=[pltpu.SemaphoreType.DMA((len(mats),))],
        compiler_params=params([], 2),
        cost_estimate=cost(0, 4 * sum(mat.size for mat in mats)),
        name="load_weights",
    )(*[far(mat) for mat in mats])


def pack_kernel(tokens, grads, far_routes, weights, out, held, turned, routes, sems):
    rows, width = tokens.shape
    pairs = ((tokens, pl.ds(0, width)), (grads, pl.ds(width + LANES, width)))
    pairs = [(part, held.at[:, band]) for part, band in pairs]
    copies = copy_all([(far_routes, routes), *pairs], sems)
    copies[0].wait()
    expert = lax.broadcasted_iota(jnp.int32, (LANES, rows), 0)
    dense = jnp.zeros((LANES, rows), F32)
    for k in range(routes.shape[0]):
        dense += jnp.where(routes[k : k + 1, :] == expert, weights[k : k + 1, :].astype(F32), 0.0)
    turned[...] = dense.astype(BF)
    held[:, width : width + LANES] = right_product(eye(rows), turned[...]).astype(BF)
    wait_all(copies[1:])
    wait_all(copy_all([(held, out)], sems))


def pack(tokens, grads, routes, weights):
    rows, width = tokens.shape
    scratch = [
        pltpu.VMEM((rows, 2 * width + LANES), BF),
        pltpu.VMEM((LANES, rows), BF),
        pltpu.VMEM(routes.T.shape, jnp.int32),
        pltpu.SemaphoreType.DMA((3,)),
    ]
    return pl.pallas_call(
        pack_kernel,
        out_shape=far_shape(rows, 2 * width + LANES),
        in_specs=[ANY, ANY, ANY, HELD],
        out_specs=ANY,
        scratch_shapes=scratch,
        compiler_params=params(scratch, 3),
        cost_estimate=cost(1e6, 8 * rows * width),
        name="pack",
    )(far(tokens), far(grads), far(routes.T), weights.T)


def pick_kernel(capacity, counts, halves, skipped, me, *refs):
    total = sum(counts)
    blocks, refs = refs[:total], refs[total + skipped :]
    rows_out, choice, refs = refs[0], refs[1], refs[2:]
    split, (held, made, sems, out_sems) = refs[:-4], refs[-4:]
    tok_rows = choice.shape[1]
    width = (held.shape[1] - LANES) // 2
    wide = width + LANES
    copies, at = [], 0
    for j, count in enumerate(counts):
        rows, low, pairs = pl.ds(j * tok_rows, tok_rows), 0, []
        for part in blocks[at : at + count]:
            pairs.append((part, held.at[rows, pl.ds(low, part.shape[1])]))
            low += part.shape[1]
        copies.append(copy_all(pairs, sems.at[j]))
        at += count
    lane = lax.broadcasted_iota(jnp.int32, (8, LANES), 1)
    mine = (lane == me[0]).astype(F32).astype(BF)
    first = lax.broadcasted_iota(jnp.int32, (tok_rows, tok_rows), 0)
    second = lax.broadcasted_iota(jnp.int32, (tok_rows, tok_rows), 1)
    earlier = (first < second).astype(F32).astype(BF)
    want = lax.broadcasted_iota(jnp.int32, (capacity, tok_rows), 0)
    sent = Outgoing(out_sems)
    for j in range(len(counts)):
        wait_all(copies[j])
        near = pl.ds(j * tok_rows, tok_rows)
        if halves:
            band = pl.ds(wide, width) if j else pl.ds(0, wide)
            sent.send(held.at[near, band], split[j])
        out = pl.ds(j * capacity, capacity)
        block = held[near, :]
        routed = right_product(mine, block[:, width:wide]) > 0
        slot = product(routed.astype(F32).astype(BF), earlier)
        slot = jnp.where(routed, slot, -1.0).astype(jnp.int32)
        pick = (want == slot[0:1, :]).astype(F32).astype(BF)
        choice[out, :] = pick
        made[out, :] = product(pick, block).astype(BF)
        sent.send(made.at[out, :], rows_out.at[out, :])
    sent.wait()


def pick_rows(me, capacity, blocks, halves=False, behind_of=()):
    counts = [len(parts) for parts in blocks]
    flat = [part for parts in blocks for part in parts]
    wide = sum(part.shape[1] for part in blocks[0])
    tok_rows = flat[0].shape[0]
    rows = capacity * len(blocks)
    width = (wide - LANES) // 2
    out_shape = [far_shape(rows, wide), shape_of(rows, tok_rows)]
    if halves:
        out_shape += [far_shape(tok_rows, width + LANES), far_shape(tok_rows, width)]
    scratch = [
        pltpu.VMEM((tok_rows * len(blocks), wide), BF),
        pltpu.VMEM((rows, wide), BF),
        pltpu.SemaphoreType.DMA((len(blocks), max(counts))),
        pltpu.SemaphoreType.DMA((len(blocks) * (2 if halves else 1),)),
    ]
    return pl.pallas_call(
        functools.partial(pick_kernel, capacity, counts, halves, len(behind_of)),
        out_shape=out_shape,
        in_specs=[SCALAR] + [ANY] * (len(flat) + len(behind_of)),
        out_specs=[ANY, HELD] + [ANY] * (len(out_shape) - 2),
        scratch_shapes=scratch,
        compiler_params=params(scratch, 3),
        cost_estimate=cost(2 * rows * tok_rows * wide, 6 * rows * wide),
        name="pick_rows",
    )(me, *flat, *behind_of)


def expert_kernel(count, capacity, blocks, halves, me, *refs):
    parts, refs = refs[:count], refs[count:]
    pick_count = count if blocks else 0
    picks, refs = refs[:pick_count], refs[pick_count:]
    gate, up, down = refs[:3]
    hidden_far, refs = refs[3:6], refs[6:]
    outs, refs = refs[: blocks + halves], refs[blocks + halves :]
    gate_out, up_out, weighted_out, rows, sems, out_sems = refs[:6]
    if blocks:
        back, dense = refs[6:]
    sent = Outgoing(out_sems)
    wait_all(copy_all(stacked(parts, rows), sems))
    width, hidden = gate.shape
    tail, grad_band = pl.ds(width, LANES), pl.ds(width + LANES, width)
    tokens, grads = rows[:, pl.ds(0, width)], rows[:, grad_band]
    lane = lax.broadcasted_iota(jnp.int32, (rows.shape[0], LANES), 1)
    scale = jnp.where(lane == me[0], rows[:, tail].astype(F32), 0.0)
    scale = jnp.sum(scale, axis=1, keepdims=True)
    prob = jnp.zeros((rows.shape[0], 1), F32)
    for low, high in spans_of(hidden):
        pre_gate = product(tokens, gate[:, low:high])
        pre_up = product(tokens, up[:, low:high])
        plain = right_product(grads, down[low:high, :])
        sigma = jax.nn.sigmoid(pre_gate)
        active = pre_gate * sigma
        held = active * pre_up
        if blocks:
            prob += jnp.sum(held.astype(BF).astype(F32) * plain, axis=1, keepdims=True)
        hidden_grad = scale * plain
        slope = pre_up * sigma * (1.0 + pre_gate * (1.0 - sigma))
        gate_out[:, low:high] = (hidden_grad * slope).astype(BF)
        up_out[:, low:high] = (hidden_grad * active).astype(BF)
        weighted_out[:, low:high] = (scale * held).astype(BF)
    for near, far_out in zip((gate_out, up_out, weighted_out), hidden_far):
        sent.send(near, far_out)
    if not blocks:
        sent.wait()
        return
    for low, high in spans_of(width):
        total = right_product(gate_out[...], gate[low:high, :])
        total = total + right_product(up_out[...], up[low:high, :])
        back[:, low:high] = total.astype(BF)
    back[:, width:] = jnp.where(lane == me[0], prob, 0.0).astype(BF)
    half = width // 2
    at, j = 0, 0
    for pick in picks:
        unit = eye(pick.shape[1])
        for first in range(0, pick.shape[0], capacity):
            turned = right_product(unit, pick[pl.ds(first, capacity), :]).astype(BF)
            dense[j] = product(turned, back[pl.ds(at + first, capacity), :]).astype(BF)
            if halves and j == blocks - 1:
                sent.send(dense.at[j, :, pl.ds(0, half)], outs[j])
                sent.send(dense.at[j, :, pl.ds(half, half + LANES)], outs[j + 1])
            else:
                sent.send(dense.at[j], outs[j])
            j += 1
        at += pick.shape[0]
    sent.wait()


def expert_rows(me, capacity, parts, mats, picks=(), halves=False):
    width, hidden = mats[0].shape
    rows = sum(part.shape[0] for part in parts)
    blocks = rows // capacity if picks else 0
    out_shape = [far_shape(rows, hidden)] * 3
    scratch = [pltpu.VMEM((rows, hidden), BF)] * 3 + [
        pltpu.VMEM((rows, parts[0].shape[1]), BF),
        pltpu.SemaphoreType.DMA((len(parts),)),
        pltpu.SemaphoreType.DMA((4 + blocks,)),
    ]
    if picks:
        tok_rows = picks[0].shape[1]
        out_shape += [far_shape(tok_rows, width + LANES)] * (blocks - halves)
        if halves:
            out_shape += [far_shape(tok_rows, width // 2 + extra) for extra in (0, LANES)]
        scratch += [
            pltpu.VMEM((rows, width + LANES), BF),
            pltpu.VMEM((blocks, tok_rows, width + LANES), BF),
        ]
    made = pl.pallas_call(
        functools.partial(expert_kernel, len(parts), capacity, blocks, halves),
        out_shape=out_shape,
        in_specs=[SCALAR] + [ANY] * len(parts) + [HELD] * (len(picks) + 3),
        out_specs=[ANY] * len(out_shape),
        scratch_shapes=scratch,
        compiler_params=params(scratch, 5),
        cost_estimate=cost((10 if picks else 6) * rows * width * hidden, 2 * rows * width),
        name="expert_rows",
    )(me, *parts, *picks, *mats)
    return made[:3], made[3:]


def add_kernel(ahead, behind, ahead_term, behind_term, *refs):
    ahead_out, behind_out, held, made, sems, out_sems = refs
    width = held.shape[2]
    bands = pl.ds(0, ahead.shape[1]), pl.ds(width - behind.shape[1], behind.shape[1])
    copies = copy_all(
        [
            (ahead, held.at[0, :, bands[0]]),
            (behind, held.at[1, :, bands[1]]),
            (ahead_term, made.at[0]),
            (behind_term, made.at[1]),
        ],
        sems,
    )
    sent = Outgoing(out_sems)
    for side, out in enumerate((ahead_out, behind_out)):
        copies[side].wait()
        copies[2 + side].wait()
        band = bands[side]
        total = made[side, :, band].astype(F32) + held[side, :, band].astype(F32)
        made[side, :, band] = total.astype(BF)
        sent.send(made.at[side], out)
    sent.wait()


def add_blocks(run, terms):
    rows, width = terms[0].shape
    scratch = [
        pltpu.VMEM((2, rows, width), BF),
        pltpu.VMEM((2, rows, width), BF),
        pltpu.SemaphoreType.DMA((4,)),
        pltpu.SemaphoreType.DMA((2,)),
    ]
    return pl.pallas_call(
        add_kernel,
        out_shape=[far_shape(rows, width)] * 2,
        in_specs=[ANY] * 4,
        out_specs=[ANY] * 2,
        scratch_shapes=scratch,
        compiler_params=params(scratch, 3),
        cost_estimate=cost(2 * rows * width, 12 * rows * width),
        name="add_blocks",
    )(*run, *terms)


def finish_kernel(routes, first, second, own, out, prob_out, held, sems):
    copies = copy_all([(part, held.at[i]) for i, part in enumerate((first, second, own))], sems)
    wait_all(copies)
    width = out.shape[1]
    total = held[0].astype(F32) + held[1].astype(F32) + held[2].astype(F32)
    out[...] = total[:, :width].astype(BF)
    tail = right_product(eye(LANES), total[:, width:].astype(BF))
    expert = lax.broadcasted_iota(jnp.int32, tail.shape, 0)
    for k in range(routes.shape[0]):
        mine = jnp.where(expert == routes[k : k + 1, :], tail, 0.0)
        prob_out[k : k + 1, :] = jnp.sum(mine, axis=0, keepdims=True).astype(BF)


def finish(routes, *parts):
    rows, width = parts[0].shape
    scratch = [
        pltpu.VMEM((len(parts), rows, width), BF),
        pltpu.SemaphoreType.DMA((len(parts),)),
    ]
    out, prob = pl.pallas_call(
        finish_kernel,
        out_shape=(shape_of(rows, width - LANES), shape_of(*routes.T.shape)),
        in_specs=[HELD] + [ANY] * len(parts),
        scratch_shapes=scratch,
        compiler_params=params(scratch, 4),
        cost_estimate=cost(3 * rows * width, 8 * rows * width),
        name="finish",
    )(routes.T, *parts)
    return out, prob.T


def share_kernel(across_count, count, offsets, copy, *refs):
    across, tiles, refs = refs[:across_count], refs[across_count : across_count + 3 * count], refs[-9:]
    out, first, second, grads, turned, made, sems, grad_sems, out_sems = refs
    share = first.shape[1]
    near, later = [], []
    for kind in range(3):
        if kind != 1:
            i, columns = (1, second) if kind else (0, first)
            low = pl.multiple_of(offsets[i] + copy[0] * share, LANES)
            near.append(copy_all(stacked(across, columns, pl.ds(low, share)), sems.at[i]))
        some = tiles[kind * count : (kind + 1) * count]
        later.append(copy_all(stacked(some, grads.at[kind]), grad_sems.at[kind]))
    sent = Outgoing(out_sems)
    for kind in range(3):
        if kind != 1:
            wait_all(near[kind // 2])
            columns = second if kind else first
            turned[...] = right_product(eye(share), columns[...]).astype(BF)
        wait_all(later[kind])
        rows = pl.ds(kind * share, share)
        for low, high in spans_of(grads.shape[2]):
            made[rows, low:high] = product(turned[...], grads[kind, :, low:high]).astype(BF)
        sent.send(made.at[rows, :], out.at[rows, :])
    sent.wait()


def share_products(copy, share, offsets, across, grads):
    rows = sum(part.shape[0] for part in across)
    hidden = grads[0][0].shape[1]
    count = len(grads[0])
    ins = [far(part) for part in (*across, *[part for kind in grads for part in kind])]
    scratch = [
        pltpu.VMEM((rows, share), BF),
        pltpu.VMEM((rows, share), BF),
        pltpu.VMEM((3, rows, hidden), BF),
        pltpu.VMEM((share, rows), BF),
        pltpu.VMEM((3 * share, hidden), BF),
        pltpu.SemaphoreType.DMA((2, len(across))),
        pltpu.SemaphoreType.DMA((3, count)),
        pltpu.SemaphoreType.DMA((3,)),
    ]
    return pl.pallas_call(
        functools.partial(share_kernel, len(across), count, offsets),
        out_shape=far_shape(3 * share, hidden),
        in_specs=[SCALAR] + [ANY] * len(ins),
        out_specs=ANY,
        scratch_shapes=scratch,
        compiler_params=params(scratch, 4),
        cost_estimate=cost(6 * rows * share * hidden, 6 * rows * hidden),
        name="share_products",
    )(copy, *ins)


def merge_kernel(kept, given, gate_out, up_out, down_out, first, second, made, turned, sems, out_sems):
    share = gate_out.shape[0]
    copies = []
    for kind in range(3):
        rows = pl.ds(kind * share, share)
        pairs = ((kept.at[rows, :], first.at[rows, :]), (given.at[rows, :], second.at[rows, :]))
        copies.append(copy_all(pairs, sems.at[kind]))
    sent = Outgoing(out_sems)
    for kind, out in enumerate((gate_out, up_out, down_out)):
        wait_all(copies[kind])
        rows = pl.ds(kind * share, share)
        made[rows, :] = (first[rows, :].astype(F32) + second[rows, :].astype(F32)).astype(BF)
        if kind < 2:
            sent.send(made.at[rows, :], out)
            continue
        for low, high in spans_of(made.shape[1]):
            turned[low:high, :] = right_product(eye(high - low), made[rows, low:high]).astype(BF)
        sent.send(turned, out)
    sent.wait()


def merge(kept, given):
    rows, hidden = kept.shape
    share = rows // 3
    shapes = ((share, hidden), (share, hidden), (hidden, share))
    scratch = [pltpu.VMEM((rows, hidden), BF)] * 3 + [
        pltpu.VMEM((hidden, share), BF),
        pltpu.SemaphoreType.DMA((3, 2)),
        pltpu.SemaphoreType.DMA((3,)),
    ]
    return pl.pallas_call(
        merge_kernel,
        out_shape=[far_shape(*shape) for shape in shapes],
        in_specs=[ANY, ANY],
        out_specs=[ANY] * 3,
        scratch_shapes=scratch,
        compiler_params=params(scratch, 4),
        cost_estimate=cost(rows * hidden, 6 * rows * hidden),
        name="merge",
    )(far(kept), given)


def body(tokens, grad_out, routes, route_weight, w_gate, w_up, w_down):
    tok_rows, model_width = tokens.shape
    route_count = routes.shape[1]
    experts = lax.axis_size("expert")
    copies = lax.axis_size("dp")
    mirrors = copies // 2
    half_ring = experts // 2
    capacity = 4 * tok_rows * route_count // (3 * experts)
    share = model_width // copies
    *mats, loaded = load_weights(w_gate[0], w_up[0], w_down[0])
    ring = ring_order(experts)
    ahead = [(ring[i], ring[(i + 1) % experts]) for i in range(experts)]
    behind = [(ring[i], ring[(i - 1) % experts]) for i in range(experts)]
    me = lax.axis_index("expert").astype(jnp.int32).reshape(1)
    copy_here = lax.axis_index("dp").astype(jnp.int32).reshape(1)

    offsets = [0]
    for step in range(1, half_ring):
        offsets += [-step, step]
    offsets.append(half_ring)
    at_offset = {offset: index for index, offset in enumerate(offsets)}

    mirror_maps = [
        [(d, (d + 2 * turn) % copies) for d in range(copies)] for turn in range(1, mirrors)
    ]
    own, others, picks = [], [[] for _ in mirror_maps], []

    def pick_blocks(blocks, *deps, **how):
        rows, pick, *split = pick_rows(me, capacity, after(blocks, *deps), **how)
        picks.append(pick)
        own.append(rows)
        for turn, pairs in enumerate(mirror_maps):
            others[turn].append(lax.ppermute(rows, "dp", pairs))
        return split

    parts, all_rows, dense = [], [], []

    def mirror_group(group, *deps):
        for taken in others:
            rows = after(taken[group], *deps)
            parts.append(expert_rows(me, capacity, rows, mats)[0])
            all_rows.extend(rows)
        return parts[-1][0]

    def expert_group(group, *deps):
        rows = [far(part) for part in after(own[group], *deps)]
        grown, back = expert_rows(me, capacity, rows, mats, picks[group], group.stop is None)
        parts.append(grown)
        all_rows.extend(rows)
        dense.extend(back)

    packed = pack(tokens, grad_out, routes, route_weight)
    pair = packed, packed
    for step in range(1, half_ring):
        run = lax.ppermute(pair[0], "expert", ahead), lax.ppermute(pair[1], "expert", behind)
        if step == 1:
            pick_blocks([(packed,)], behind_of=(loaded,))
        else:
            pick_blocks([(block,) for block in pair])
        done = picks[-1]
        if step == 2:
            expert_group(slice(0, 2))
            done = dense[0]
        if step == half_ring - 1:
            expert_group(slice(2, step))
            done = mirror_group(slice(0, step - 1), dense[-1])
        if step > 1:
            done = done, [taken[step - 2] for taken in others]
        pair = lax.optimization_barrier((run, done))[0]
    split = pick_blocks([(block,) for block in pair], halves=True)
    last = (lax.ppermute(split[0], "expert", ahead), lax.ppermute(split[1], "expert", behind))
    expert_group(slice(half_ring - 1, half_ring))
    pick_blocks([last], dense[-1])
    expert_group(slice(half_ring, None))

    core_pairs = [(d, d ^ 1) for d in range(copies)]

    def shares(copy, *deps):
        grads = [[part[kind] for part in parts] for kind in range(3)]
        offsets = (0, model_width + LANES)
        return share_products(after(copy, *deps), share, offsets, all_rows, grads)

    run = dense[-2:]
    before = run[0]
    for step in range(half_ring - 1, -1, -1):
        run = lax.ppermute(run[0], "expert", ahead), lax.ppermute(run[1], "expert", behind)
        if step == 0:
            break
        if step == half_ring - 1:
            before = before, mirror_group(slice(step - 1, step), before)
        elif step == half_ring - 2:
            before = before, mirror_group(slice(half_ring - 1, None), before)
        elif step == half_ring - 3:
            sent_share = shares(copy_here ^ 1, before)
            before = before, sent_share
        run = add_blocks(after(run, before), [dense[at_offset[sign * step]] for sign in (1, -1)])
        before = run[0]
    given = lax.ppermute(after(sent_share, before), "dp", core_pairs)
    kept = shares(copy_here, before)
    merged = merge(kept, given)
    token_grad, prob_out = finish(routes, *after(run, merged[0]), dense[0])
    wgrads = [part[None] for part in merged]
    return (token_grad, prob_out, *wgrads)


def solution(mesh):
    in_specs = (
        P(("dp", "expert"), None),
        P(("dp", "expert"), None),
        P(("dp", "expert"), None),
        P(("dp", "expert"), None),
        P("expert", None, None),
        P("expert", None, None),
        P("expert", None, None),
    )
    out_specs = (
        P(("dp", "expert"), None),
        P(("dp", "expert"), None),
        P("expert", "dp", None),
        P("expert", "dp", None),
        P("expert", None, "dp"),
    )
    return jax.shard_map(body, mesh=mesh, in_specs=in_specs, out_specs=out_specs, check_vma=False)
```
